512 devices in a mesh: slab: 128 (over z, y, core), col: 4 (over x).
Axes of the slice: x: 4, y: 4, z: 16, core: 2. Of those that a mesh axis runs over, the one named last changes fastest.
Arguments:
- stiff_tiles: float32 [4096, 3, 128, 128], P('slab'), as said below
- tile_mask: int32 [4096, 2], P('slab'), may hold values from 0 to 1, as said below
- edge_star: float32 [524288], P('slab'), may hold values from 0.5 to 2
- start_modes: float32 [16, 524288], P(None, 'slab'), may hold values from -6 to 6
- start_directions: float32 [16, 524288], P(None, 'slab'), may hold values from -6 to 6
Outputs:
- mode_block: float32 [16, 524288], P(None, 'slab')
- directions: float32 [16, 524288], P(None, 'slab')
- ritz: float32 [16, 16], replicated
The draws below stay inside these ranges and needn't reach their ends.
Inputs may be any that keep to these rules, and one draw needn't show every extreme that they name: The assembled operator is symmetric and positive definite: stiff_tiles[b, 0] is the transpose of stiff_tiles[b - 1, 2] and stiff_tiles[b, 1] is symmetric. tile_mask[b, 0] equals tile_mask[b - 1, 1] for b of 1 and more.
All inputs are finite; a program needn't handle non-finite values.
Results may differ from the reference program's by a relative error of at most 0.0003.
Values sent between devices are 32-bit elements; how exact they have to be, the bound alone decides.
No kernel may reach another device: no remote copies, remote signals or barrier semaphores. Data moves between devices by JAX's collectives and lax.ppermute only.
A program may use at most 64 MiB of HBM per device.

```python
import math
import jax
import jax.numpy as jnp
from jax import lax

MODES = 16
TILE = 128
ITERS = 3
ROWS = 524288


def draw_stiff_tiles(key, part):
    key_couple = jax.random.fold_in(key, 11)
    key_inner = jax.random.fold_in(key, 12)
    key_diag = jax.random.fold_in(key, 13)
    nblocks = ROWS // TILE
    limit = 0.9 * float(TILE) ** (-0.5)
    coupling = jax.random.uniform(key_couple, (nblocks, TILE, TILE), jnp.float32, -limit, limit)
    diagonal = 6.0 + 6.0 * jax.random.uniform(key_diag, (nblocks, TILE), jnp.float32)
    inner = jax.random.uniform(key_inner, (nblocks, TILE, TILE), jnp.float32, -limit, limit)
    inner = 0.5 * (inner + jnp.transpose(inner, (0, 2, 1)))
    identity = jnp.eye(TILE, dtype=jnp.float32)[None]
    middle = inner * (1.0 - identity) + identity * diagonal[:, :, None]
    lower = jnp.transpose(jnp.roll(coupling, 1, axis=0), (0, 2, 1))
    return jnp.stack([lower, middle, coupling], axis=1)


def draw_tile_mask(key, part):
    nblocks = ROWS // TILE
    present = jnp.minimum(jax.random.randint(jax.random.fold_in(key, 21), (nblocks,), 0, 4), 1).astype(jnp.int32)
    return jnp.stack([jnp.roll(present, 1), present], axis=1)


def level_of(rng, shape, pieces, least, largest):
    loudness = 1.0
    for position, shards_of in pieces:
        steps = jax.random.uniform(jax.random.fold_in(jax.random.fold_in(rng, 6), position), (shards_of,), jnp.float32, least / len(pieces), largest / len(pieces))
        loudness = loudness * jnp.repeat(jnp.exp(steps), shape[position] // shards_of).reshape((-1,) + (1,) * (len(shape) - 1 - position))
    return loudness


def bell_draw(own_key, extent, spread, bound, pieces=(), kind=jnp.bfloat16):
    values = spread * jax.random.normal(own_key, extent, jnp.float32)
    if pieces:
        values = values * level_of(own_key, extent, pieces, -0.22, 0.18)
    return jnp.clip(values, -bound, bound).astype(kind)


def setup_inputs(seed: int = 0) -> dict:
    seeds = jax.random.split(jax.random.key(seed), 6)
    return {
        "stiff_tiles": draw_stiff_tiles(jax.random.fold_in(seeds[5], 71), 0),
        "tile_mask": draw_tile_mask(jax.random.fold_in(seeds[5], 71), 0),
        "edge_star": jnp.clip(jnp.exp(math.log(2.0) - 1.3862944 * jax.random.uniform(seeds[2], (ROWS,), jnp.float32) ** level_of(seeds[2], (ROWS,), ((0, 128),), -0.2, 0.2)), 0.5, 2.0),
        "start_modes": bell_draw(seeds[3], (MODES, ROWS), 1.0, 6.0, ((1, 128),), jnp.float32),
        "start_directions": bell_draw(seeds[4], (MODES, ROWS), 1.0, 6.0, ((1, 128),), jnp.float32),
    }


def band_product(tile_set, coupling, padded_blocks):
    nblocks = tile_set.shape[0]
    lower_term = jnp.einsum('bij,cbj->cbi', tile_set[:, 0], padded_blocks[:, 0:nblocks], precision=lax.Precision.HIGHEST)
    middle_term = jnp.einsum('bij,cbj->cbi', tile_set[:, 1], padded_blocks[:, 1:nblocks + 1], precision=lax.Precision.HIGHEST)
    upper_term = jnp.einsum('bij,cbj->cbi', tile_set[:, 2], padded_blocks[:, 2:nblocks + 2], precision=lax.Precision.HIGHEST)
    weight_low = coupling[:, 0].astype(jnp.float32)[None, :, None]
    weight_high = coupling[:, 1].astype(jnp.float32)[None, :, None]
    return lower_term * weight_low + middle_term + upper_term * weight_high

def operate(field, tile_set, coupling):
    tile_width = tile_set.shape[-1]
    padded = jnp.pad(field, ((0, 0), (tile_width, tile_width)))
    shaped = padded.reshape(field.shape[0], -1, tile_width)
    return band_product(tile_set, coupling, shaped).reshape(field.shape[0], -1)

def cross_gram(left, right):
    return lax.dot_general(left.astype(jnp.float32), right.astype(jnp.float32), (((1,), (1,)), ((), ())), precision=lax.Precision.HIGHEST, preferred_element_type=jnp.float32)

def product(left, right):
    return jnp.dot(left.astype(jnp.float32), right.astype(jnp.float32), precision=lax.Precision.HIGHEST, preferred_element_type=jnp.float32)

def symmetric(matrix):
    return 0.5 * (matrix + matrix.T)

def rayleigh_ritz(gram_stiff, gram_mass, total_rows, mode_count):
    shifted = gram_stiff + 1.0 * gram_mass
    factor = jnp.linalg.cholesky(shifted)
    coeffs = jax.scipy.linalg.cho_solve((factor, True), gram_mass[:, :mode_count])
    normalizer = product(coeffs.T, product(gram_mass, coeffs)) / total_rows
    chol_factor = jnp.linalg.cholesky(normalizer)
    rotation = jax.scipy.linalg.solve_triangular(chol_factor, coeffs.T, lower=True)
    ritz_matrix = product(rotation, product(gram_stiff, rotation.T)) / total_rows
    return (rotation, ritz_matrix)

def reference(stiff_tiles, tile_mask, edge_star, start_modes, start_directions):
    star_row = edge_star[None, :]
    both_blocks = jnp.concatenate([start_modes, start_directions], axis=0)
    applied = operate(both_blocks, stiff_tiles, tile_mask)
    mode_applied = applied[:MODES]
    dir_applied = applied[MODES:]
    gram_mass = symmetric(cross_gram(start_modes, start_modes * star_row))
    gram_stiff = symmetric(cross_gram(start_modes, mode_applied))
    chol_factor = jnp.linalg.cholesky(gram_mass / ROWS)
    rotation = jax.scipy.linalg.solve_triangular(chol_factor, jnp.eye(MODES, dtype=jnp.float32), lower=True)
    mode_block = product(rotation, start_modes)
    mode_applied = product(rotation, mode_applied)
    ritz_matrix = product(rotation, product(gram_stiff, rotation.T)) / ROWS
    directions = start_directions
    for iteration in range(ITERS):
        residual = mode_applied - product(ritz_matrix, mode_block * star_row)
        res_applied = operate(residual, stiff_tiles, tile_mask)
        stacked = jnp.concatenate([mode_block, residual, directions], axis=0)
        applied_stack = jnp.concatenate([mode_applied, res_applied, dir_applied], axis=0)
        gram_stiff = symmetric(cross_gram(stacked, applied_stack))
        gram_mass = symmetric(cross_gram(stacked, stacked * star_row))
        rotation, ritz_matrix = rayleigh_ritz(gram_stiff, gram_mass, ROWS, MODES)
        mode_block = product(rotation, stacked)
        mode_applied = product(rotation, applied_stack)
        tail_rotation = rotation[:, MODES:]
        directions = product(tail_rotation, stacked[MODES:])
        dir_applied = product(tail_rotation, applied_stack[MODES:])
    return (mode_block, directions, ritz_matrix)
```

```python
import jax
import jax.numpy as jnp
from jax import lax
from jax.sharding import Mesh
from jax.sharding import PartitionSpec as P

ITERS = 3
SLAB = ("z", "y", "core")


def slab_sum(rows):
    parts = lax.axis_size(("y", "core"))
    shared = rows.reshape(parts, -1, 128)
    own = lax.all_to_all(shared, ("y", "core"), 0, 0, tiled=True).sum(0)
    copies = jnp.broadcast_to(own[None], (lax.axis_size("z"),) + own.shape)
    own = lax.all_to_all(copies, "z", 0, 0, tiled=True).sum(0)
    copies = jnp.broadcast_to(own[None], (parts,) + own.shape)
    return lax.all_to_all(copies, ("y", "core"), 0, 0, tiled=True).reshape(rows.shape)


def summed_pair(first, second):
    count = first.size
    flat = jnp.concatenate([first.reshape(-1), second.reshape(-1)])
    flat = jnp.pad(flat, (0, -flat.size % 1024)).reshape(-1, 128)
    flat = slab_sum(flat).reshape(-1)
    return flat[:count].reshape(first.shape), flat[count : 2 * count].reshape(second.shape)


def extended(block, sides, width):
    for axis, dim in sides:
        count = lax.axis_size(axis)
        forward = [(i, i + 1) for i in range(count - 1)]
        backward = [(target, source) for source, target in forward]
        low = lax.ppermute(
            lax.slice_in_dim(block, block.shape[dim] - width, None, axis=dim), axis, forward
        )
        high = lax.ppermute(lax.slice_in_dim(block, 0, width, axis=dim), axis, backward)
        block = jnp.concatenate([low, block, high], axis=dim)
    return block


def band_product(tile_set, coupling, padded_blocks):
    nblocks = tile_set.shape[0]
    lower_term = jnp.einsum(
        "bij,cbj->cbi", tile_set[:, 0], padded_blocks[:, 0:nblocks], precision=lax.Precision.HIGHEST
    )
    middle_term = jnp.einsum(
        "bij,cbj->cbi",
        tile_set[:, 1],
        padded_blocks[:, 1 : nblocks + 1],
        precision=lax.Precision.HIGHEST,
    )
    upper_term = jnp.einsum(
        "bij,cbj->cbi",
        tile_set[:, 2],
        padded_blocks[:, 2 : nblocks + 2],
        precision=lax.Precision.HIGHEST,
    )
    weight_low = coupling[:, 0].astype(jnp.float32)[None, :, None]
    weight_high = coupling[:, 1].astype(jnp.float32)[None, :, None]
    return lower_term * weight_low + middle_term + upper_term * weight_high


def operate(field, tile_set, coupling):
    tile_width = tile_set.shape[-1]
    count = field.shape[0]
    padded = extended(field, ((SLAB, 1),), tile_width)
    shaped = padded.reshape(count, -1, tile_width)
    return band_product(tile_set, coupling, shaped).reshape(count, -1)


def cross_gram(left, right):
    return lax.dot_general(
        left,
        right,
        (((1,), (1,)), ((), ())),
        precision=lax.Precision.HIGHEST,
        preferred_element_type=jnp.float32,
    )


def product(left, right):
    return jnp.dot(left, right, precision=lax.Precision.HIGHEST, preferred_element_type=jnp.float32)


def symmetric(matrix):
    return 0.5 * (matrix + matrix.T)


def projections(stacked, applied_stack, star_row):
    gram_stiff, gram_mass = summed_pair(
        cross_gram(stacked, applied_stack), cross_gram(stacked, stacked * star_row)
    )
    return (symmetric(gram_stiff), symmetric(gram_mass))


def rayleigh_ritz(gram_stiff, gram_mass, total_rows, mode_count):
    shifted = gram_stiff + 1.0 * gram_mass
    factor = jnp.linalg.cholesky(shifted)
    coeffs = jax.scipy.linalg.cho_solve((factor, True), gram_mass[:, :mode_count])
    normalizer = product(coeffs.T, product(gram_mass, coeffs)) / total_rows
    chol_factor = jnp.linalg.cholesky(normalizer)
    rotation = jax.scipy.linalg.solve_triangular(chol_factor, coeffs.T, lower=True)
    ritz_matrix = product(rotation, product(gram_stiff, rotation.T)) / total_rows
    return (rotation, ritz_matrix)


def on_device(stiff_tiles, tile_mask, edge_star, start_modes, start_directions):
    mode_count = start_modes.shape[0]
    total_rows = edge_star.shape[0] * lax.axis_size(SLAB)
    star_row = edge_star[None, :]
    both_blocks = jnp.concatenate([start_modes, start_directions], axis=0)
    applied = operate(both_blocks, stiff_tiles, tile_mask)
    mode_applied = applied[:mode_count]
    dir_applied = applied[mode_count:]
    start_mass, start_stiff = summed_pair(
        cross_gram(start_modes, start_modes * star_row), cross_gram(start_modes, mode_applied)
    )
    chol_factor = jnp.linalg.cholesky(symmetric(start_mass) / total_rows)
    rotation = jax.scipy.linalg.solve_triangular(
        chol_factor, jnp.eye(mode_count, dtype=jnp.float32), lower=True
    )
    mode_block = product(rotation, start_modes)
    mode_applied = product(rotation, mode_applied)
    ritz_matrix = product(rotation, product(symmetric(start_stiff), rotation.T)) / total_rows
    directions = start_directions
    for iteration in range(ITERS):
        residual = mode_applied - product(ritz_matrix, mode_block * star_row)
        res_applied = operate(residual, stiff_tiles, tile_mask)
        stacked = jnp.concatenate([mode_block, residual, directions], axis=0)
        applied_stack = jnp.concatenate([mode_applied, res_applied, dir_applied], axis=0)
        gram_stiff, gram_mass = projections(stacked, applied_stack, star_row)
        rotation, ritz_matrix = rayleigh_ritz(gram_stiff, gram_mass, total_rows, mode_count)
        mode_block = product(rotation, stacked)
        mode_applied = product(rotation, applied_stack)
        tail_rotation = rotation[:, mode_count:]
        directions = product(tail_rotation, stacked[mode_count:])
        dir_applied = product(tail_rotation, applied_stack[mode_count:])
    return (mode_block, directions, ritz_matrix)


def solution(mesh):
    fine = Mesh(mesh.devices.reshape(-1, 4, 2, 4), ("z", "y", "core", "x"))
    in_specs = (
        P(SLAB, None, None, None),
        P(SLAB, None),
        P(SLAB),
        P(None, SLAB),
        P(None, SLAB),
    )
    out_specs = (P(None, SLAB), P(None, SLAB), P())
    return jax.shard_map(
        on_device, mesh=fine, in_specs=in_specs, out_specs=out_specs, check_vma=False
    )
```

```python
import jax
import jax.numpy as jnp
from jax import lax
from jax.experimental import pallas as pl
from jax.experimental.pallas import tpu as pltpu
from jax.sharding import Mesh
from jax.sharding import PartitionSpec as P

SLAB = ("z", "y", "core")
TILE = 128
STEP_BLOCKS = 4


def slab_sum(rows):
    parts = lax.axis_size(("y", "core"))
    shared = rows.reshape(parts, -1, 128)
    own = lax.all_to_all(shared, ("y", "core"), 0, 0, tiled=True).sum(0)
    copies = jnp.broadcast_to(own[None], (lax.axis_size("z"),) + own.shape)
    own = lax.all_to_all(copies, "z", 0, 0, tiled=True).sum(0)
    copies = jnp.broadcast_to(own[None], (parts,) + own.shape)
    return lax.all_to_all(copies, ("y", "core"), 0, 0, tiled=True).reshape(rows.shape)


def from_left(edge):
    count = lax.axis_size(SLAB)
    return lax.ppermute(edge, SLAB, [(i, i + 1) for i in range(count - 1)])


def from_right(edge):
    count = lax.axis_size(SLAB)
    return lax.ppermute(edge, SLAB, [(i + 1, i) for i in range(count - 1)])


def with_halo(block):
    low = from_left(block[:, -TILE:])
    high = from_right(block[:, :TILE])
    return jnp.concatenate([low, block, high], axis=1)


def split(values):
    high = values.astype(jnp.bfloat16)
    low = (values - high.astype(jnp.float32)).astype(jnp.bfloat16)
    return high, low


def band_kernel(mask_ref, tiles_ref, ext_ref, out_ref):
    step = pl.program_id(0)
    count = ext_ref.shape[0]
    start = pl.multiple_of(step * STEP_BLOCKS * TILE, TILE)
    window = ext_ref[:, pl.ds(start, (STEP_BLOCKS + 2) * TILE)]
    left = jnp.concatenate(split(window), axis=0)
    for k in range(STEP_BLOCKS):
        block = step * STEP_BLOCKS + k
        weight_low = mask_ref[block, 0].astype(jnp.float32)
        weight_high = mask_ref[block, 1].astype(jnp.float32)
        row = jnp.concatenate(
            [tiles_ref[k, 0] * weight_low, tiles_ref[k, 1], tiles_ref[k, 2] * weight_high], axis=1
        )
        right = jnp.concatenate(split(row), axis=0)
        term = lax.dot_general(
            left[:, k * TILE : (k + 3) * TILE],
            right,
            (((1,), (1,)), ((), ())),
            preferred_element_type=jnp.float32,
        )
        term = term[:, :TILE] + term[:, TILE:]
        out_ref[:, k * TILE : (k + 1) * TILE] = term[:count] + term[count:]


def band(extended, tile_set, coupling):
    count, width = extended.shape
    width -= 2 * TILE
    return pl.pallas_call(
        band_kernel,
        grid=(width // (STEP_BLOCKS * TILE),),
        in_specs=[
            pl.BlockSpec(memory_space=pltpu.SMEM),
            pl.BlockSpec((STEP_BLOCKS, 3, TILE, TILE), lambda i: (i, 0, 0, 0)),
            pl.BlockSpec((count, width + 2 * TILE), lambda i: (0, 0)),
        ],
        out_specs=pl.BlockSpec((count, STEP_BLOCKS * TILE), lambda i: (0, i)),
        out_shape=jax.ShapeDtypeStruct((count, width), jnp.float32),
        compiler_params=pltpu.CompilerParams(vmem_limit_bytes=32 * 1024 * 1024),
        name="band",
    )(coupling, tile_set, extended)


def gram(left, right):
    return lax.dot_general(
        left,
        right,
        (((1,), (1,)), ((), ())),
        precision=lax.Precision.HIGHEST,
        preferred_element_type=jnp.float32,
    )


def product(left, right):
    return jnp.dot(left, right, precision=lax.Precision.HIGHEST, preferred_element_type=jnp.float32)


def symmetric(matrix):
    return 0.5 * (matrix + matrix.T)


def congruence(coeffs, matrix):
    return symmetric(product(coeffs, gram(matrix, coeffs)))


def rayleigh_ritz(gram_stiff, gram_mass, total_rows, mode_count):
    shifted = gram_stiff + 1.0 * gram_mass
    factor = jnp.linalg.cholesky(shifted)
    coeffs = jax.scipy.linalg.cho_solve((factor, True), gram_mass[:, :mode_count])
    normalizer = product(coeffs.T, product(gram_mass, coeffs)) / total_rows
    chol_factor = jnp.linalg.cholesky(normalizer)
    rotation = jax.scipy.linalg.solve_triangular(chol_factor, coeffs.T, lower=True)
    ritz_matrix = product(rotation, product(gram_stiff, rotation.T)) / total_rows
    return (rotation, ritz_matrix)


def first_coefficients(gram_stiff, gram_mass, total_rows, m):
    eye = jnp.eye(m, dtype=jnp.float32)
    none = jnp.zeros((m, m), jnp.float32)
    chol_factor = jnp.linalg.cholesky(gram_mass[:m, :m] / total_rows)
    start = jax.scipy.linalg.solve_triangular(chol_factor, eye, lower=True)
    ritz_matrix = product(start, product(gram_stiff[:m, :m], start.T)) / total_rows
    basis = jnp.concatenate(
        [
            jnp.concatenate([start, none, none, none], axis=1),
            jnp.concatenate([none, start, -product(ritz_matrix, start), none], axis=1),
            jnp.concatenate([none, none, none, eye], axis=1),
        ]
    )
    rotation, ritz_matrix = rayleigh_ritz(
        congruence(basis, gram_stiff), congruence(basis, gram_mass), total_rows, m
    )
    modes = product(rotation, basis)
    directions = product(rotation[:, m:], basis[m:])
    return jnp.concatenate([modes, directions]), ritz_matrix


def last_coefficients(gram_stiff, gram_mass, ritz_matrix, total_rows, m):
    none = jnp.zeros((m, m), jnp.float32)
    rotation, next_ritz = rayleigh_ritz(
        gram_stiff[: 3 * m, : 3 * m], gram_mass[: 3 * m, : 3 * m], total_rows, m
    )
    of_x, of_r, of_p = rotation[:, :m], rotation[:, m : 2 * m], rotation[:, 2 * m :]
    pulled = product(next_ritz, rotation)
    zeros5 = jnp.zeros((m, 5 * m), jnp.float32)
    basis = jnp.concatenate(
        [
            jnp.concatenate([rotation, zeros5], axis=1),
            jnp.concatenate(
                [
                    none,
                    of_x,
                    none,
                    of_r,
                    of_p,
                    product(of_x, ritz_matrix) - pulled[:, :m],
                    -pulled[:, m:],
                ],
                axis=1,
            ),
            jnp.concatenate([none, of_r, of_p, zeros5], axis=1),
        ]
    )
    rotation, last_ritz = rayleigh_ritz(
        congruence(basis, gram_stiff), congruence(basis, gram_mass), total_rows, m
    )
    modes = product(rotation, basis)
    directions = product(rotation[:, m:], basis[m:])
    return jnp.concatenate([modes, directions]), last_ritz


def packed(gram_stiff, gram_mass):
    size = gram_stiff.shape[0]
    low = jnp.tril(jnp.ones((size, size), bool), -1)
    both = jnp.where(low, gram_stiff, gram_mass)
    return jnp.concatenate([both, jnp.broadcast_to(jnp.diagonal(gram_stiff)[None], (8, size))])


def unpacked(rows):
    size = rows.shape[1]
    both, diagonal = rows[:size], rows[size]
    low = jnp.tril(both, -1)
    high = jnp.triu(both, 1)
    return low + low.T + jnp.diag(diagonal), high + high.T + jnp.diag(jnp.diagonal(both))


def on_device(stiff_tiles, tile_mask, edge_star, start_modes, start_directions):
    m = start_modes.shape[0]
    total_rows = edge_star.shape[0] * lax.axis_size(SLAB)
    star = edge_star[None, :]
    fields = jnp.concatenate(
        [start_modes, start_directions, start_modes * star, jnp.broadcast_to(star, (8, star.shape[1]))]
    )
    fields = with_halo(fields)
    modes, directions, mass_modes = fields[:m], fields[m : 2 * m], fields[2 * m : 3 * m]
    star_ext = fields[3 * m : 3 * m + 1]
    applied = band(fields[: 3 * m], stiff_tiles, tile_mask)
    applied_modes = with_halo(applied[:m])
    twice = band(applied_modes, stiff_tiles, tile_mask)

    basis = jnp.concatenate([modes, applied_modes, mass_modes, directions])
    own = basis[:, TILE:-TILE]
    rest = jnp.concatenate([twice, applied[2 * m : 3 * m], applied[m : 2 * m]])
    applied_own = jnp.concatenate([applied[:m], rest])
    gram_stiff = gram(own, applied_own)
    gram_mass = gram(own, own * star)
    sums = slab_sum(jnp.concatenate([symmetric(gram_stiff), symmetric(gram_mass)], axis=1))
    applied_basis = jnp.concatenate([applied_modes, with_halo(rest)])
    size = 4 * m
    coeffs, ritz_matrix = first_coefficients(sums[:, :size], sums[:, size:], total_rows, m)

    pair = product(coeffs, basis)
    applied_pair = product(coeffs, applied_basis)
    modes, directions = pair[:m], pair[m:]
    mass_modes = modes * star_ext
    residual = applied_pair[:m] - product(ritz_matrix, mass_modes)
    fields = jnp.concatenate(
        [residual, applied_pair[m:], mass_modes, residual * star_ext, directions * star_ext]
    )
    applied = band(fields, stiff_tiles, tile_mask)
    applied_residual = applied[:m]
    twice = band(with_halo(applied_residual), stiff_tiles, tile_mask)
    inner = slice(TILE, -TILE)
    own = jnp.concatenate(
        [
            modes[:, inner],
            residual[:, inner],
            directions[:, inner],
            applied_residual,
            fields[m:, inner],
        ]
    )
    applied_own = jnp.concatenate(
        [applied_pair[:m, inner], applied_residual, applied_pair[m:, inner], twice, applied[m:]]
    )
    gram_stiff = symmetric(gram(own, applied_own))
    gram_mass = symmetric(gram(own, own * star))
    gram_stiff, gram_mass = unpacked(slab_sum(packed(gram_stiff, gram_mass)))
    coeffs, ritz_matrix = last_coefficients(gram_stiff, gram_mass, ritz_matrix, total_rows, m)
    result = product(coeffs, own)
    return (result[:m], result[m:], ritz_matrix)


def solution(mesh):
    fine = Mesh(mesh.devices.reshape(-1, 4, 2, 4), ("z", "y", "core", "x"))
    in_specs = (
        P(SLAB, None, None, None),
        P(SLAB, None),
        P(SLAB),
        P(None, SLAB),
        P(None, SLAB),
    )
    out_specs = (P(None, SLAB), P(None, SLAB), P())
    return jax.shard_map(
        on_device, mesh=fine, in_specs=in_specs, out_specs=out_specs, check_vma=False
    )
```

```python
import functools

import jax
import jax.numpy as jnp
from jax import lax
from jax.experimental import pallas as pl
from jax.experimental.pallas import tpu as pltpu
from jax.sharding import Mesh
from jax.sharding import PartitionSpec as P

SLAB = ("z", "y", "core")
TILE = 128
STEP_BLOCKS = 4
WIDTH = 4


def slab_sum(rows):
    parts = lax.axis_size(("y", "core"))
    shared = rows.reshape(parts, -1, 128)
    own = lax.all_to_all(shared, ("y", "core"), 0, 0, tiled=True).sum(0)
    copies = jnp.broadcast_to(own[None], (lax.axis_size("z"),) + own.shape)
    own = lax.all_to_all(copies, "z", 0, 0, tiled=True).sum(0)
    copies = jnp.broadcast_to(own[None], (parts,) + own.shape)
    return lax.all_to_all(copies, ("y", "core"), 0, 0, tiled=True).reshape(rows.shape)


def from_left(edge):
    count = lax.axis_size(SLAB)
    return lax.ppermute(edge, SLAB, [(i, i + 1) for i in range(count - 1)])


def from_right(edge):
    count = lax.axis_size(SLAB)
    return lax.ppermute(edge, SLAB, [(i + 1, i) for i in range(count - 1)])


def with_halo(block):
    low = from_left(block[:, -TILE:])
    high = from_right(block[:, :TILE])
    return jnp.concatenate([low, block, high], axis=1)


def split(values):
    high = values.astype(jnp.bfloat16)
    low = (values - high.astype(jnp.float32)).astype(jnp.bfloat16)
    return high, low


def band_kernel(mask_ref, tiles_ref, ext_ref, out_ref):
    step = pl.program_id(0)
    count = ext_ref.shape[0]
    start = pl.multiple_of(step * STEP_BLOCKS * TILE, TILE)
    window = ext_ref[:, pl.ds(start, (STEP_BLOCKS + 2) * TILE)]
    left = jnp.concatenate(split(window), axis=0)
    for k in range(STEP_BLOCKS):
        block = step * STEP_BLOCKS + k
        weight_low = mask_ref[block, 0].astype(jnp.float32)
        weight_high = mask_ref[block, 1].astype(jnp.float32)
        row = jnp.concatenate(
            [tiles_ref[k, 0] * weight_low, tiles_ref[k, 1], tiles_ref[k, 2] * weight_high], axis=1
        )
        right = jnp.concatenate(split(row), axis=0)
        term = lax.dot_general(
            left[:, k * TILE : (k + 3) * TILE],
            right,
            (((1,), (1,)), ((), ())),
            preferred_element_type=jnp.float32,
        )
        term = term[:, :TILE] + term[:, TILE:]
        out_ref[:, k * TILE : (k + 1) * TILE] = term[:count] + term[count:]


def band(extended, tile_set, coupling):
    count, width = extended.shape
    width -= 2 * TILE
    return pl.pallas_call(
        band_kernel,
        grid=(width // (STEP_BLOCKS * TILE),),
        in_specs=[
            pl.BlockSpec(memory_space=pltpu.SMEM),
            pl.BlockSpec((STEP_BLOCKS, 3, TILE, TILE), lambda i: (i, 0, 0, 0)),
            pl.BlockSpec((count, width + 2 * TILE), lambda i: (0, 0)),
        ],
        out_specs=pl.BlockSpec((count, STEP_BLOCKS * TILE), lambda i: (0, i)),
        out_shape=jax.ShapeDtypeStruct((count, width), jnp.float32),
        compiler_params=pltpu.CompilerParams(vmem_limit_bytes=32 * 1024 * 1024),
        name="band",
    )(coupling, tile_set, extended)


def gram(left, right):
    return lax.dot_general(
        left,
        right,
        (((1,), (1,)), ((), ())),
        precision=lax.Precision.HIGHEST,
        preferred_element_type=jnp.float32,
    )


def product(left, right):
    return jnp.dot(left, right, precision=lax.Precision.HIGHEST, preferred_element_type=jnp.float32)


def symmetric(matrix):
    return 0.5 * (matrix + matrix.T)


def nn(left, right):
    return jnp.dot(left, right, precision=lax.Precision.HIGHEST, preferred_element_type=jnp.float32)


def nt(left, right):
    return gram(left, right)


def lanes(rows):
    return lax.broadcasted_iota(jnp.int32, (rows, 128), 1)


def sublanes(rows):
    return lax.broadcasted_iota(jnp.int32, (rows, 128), 0)


def diagonal(rows, shift):
    return jnp.where(lanes(rows) == sublanes(rows) + shift, 1.0, 0.0).astype(jnp.float32)


def below(matrix, limit):
    return jnp.where(lanes(matrix.shape[0]) < limit, matrix, 0.0)


def pivots(groups, first, lane, width):
    columns = [
        [jnp.broadcast_to(g[:, lane + j : lane + j + 1], (8, 128)) for g in groups]
        for j in range(width)
    ]

    def spread(values, row):
        return jnp.broadcast_to(values[row // 8][row % 8 : row % 8 + 1], (8, 128))

    block = [[spread(columns[j], first + i) for j in range(width)] for i in range(width)]
    rows = [spread(groups, first + i) for i in range(width)]
    return columns, block, rows


def solved(block, rows):
    width = len(rows)
    block, rows = [list(r) for r in block], list(rows)
    for i in range(width):
        scale = 1.0 / block[i][i]
        block[i] = [v * scale for v in block[i]]
        rows[i] = rows[i] * scale
        for k in range(width):
            if k != i:
                factor = block[k][i]
                for j in range(i + 1, width):
                    block[k][j] = block[k][j] - factor * block[i][j]
                rows[k] = rows[k] - factor * rows[i]
    return rows


def inverse(matrix, size):
    matrix = matrix + diagonal(size, 64)
    groups = [matrix[8 * t : 8 * t + 8] for t in range(size // 8)]
    row = sublanes(8)
    for first in range(0, size, WIDTH):
        columns, block, rows = pivots(groups, first, first, WIDTH)
        rows = solved(block, rows)
        for t in range(size // 8):
            for j in range(WIDTH):
                groups[t] = groups[t] - columns[j][t] * rows[j]
            for j in range(WIDTH):
                if t == (first + j) // 8:
                    groups[t] = jnp.where(row == (first + j) % 8, rows[j], groups[t])
    return jnp.concatenate(groups, axis=0)


def lower_solved(matrix, size, scale):
    groups = [matrix[8 * t : 8 * t + 8] for t in range(size // 8)]
    row = sublanes(8)
    result = [jnp.zeros((8, 128), jnp.float32) for _ in groups]
    for first in range(0, size, WIDTH):
        columns, block, rows = pivots(groups, first, 64 + first, WIDTH)
        whole = solved(block, rows)
        for i in range(WIDTH):
            inverse_root = lax.rsqrt(block[i][i]) * scale
            t, at = (first + i) // 8, (first + i) % 8
            result[t] = jnp.where(row == at, rows[i] * inverse_root, result[t])
            if i + 1 < WIDTH:
                turn = 1.0 / block[i][i]
                for k in range(i + 1, WIDTH):
                    factor = block[k][i] * turn
                    block[k] = [a - factor * b for a, b in zip(block[k], block[i])]
                    rows[k] = rows[k] - factor * rows[i]
        for t in range(size // 8):
            if 8 * t + 7 >= first + WIDTH:
                for j in range(WIDTH):
                    groups[t] = groups[t] - columns[j][t] * whole[j]
    return jnp.concatenate(result, axis=0)


def projected(basis, matrix):
    tall = jnp.concatenate([basis, jnp.zeros((80, 128), jnp.float32)], axis=0)
    return nt(nn(basis[:, : matrix.shape[0]], matrix), tall)


def rayleigh_ritz(gram_stiff, gram_mass, total_rows):
    m, n = 16, 48
    inverted = inverse(gram_stiff + 1.0 * gram_mass, n)
    coeffs = below(pltpu.roll(nn(gram_mass[:m, :n], inverted), 64, 1), n)
    padded = jnp.concatenate(
        [jnp.zeros((64, 128), jnp.float32), coeffs, jnp.zeros((48, 128), jnp.float32)], axis=0
    )
    normalizer = nt(nn(coeffs[:, :n], gram_mass), padded)
    rotation = lower_solved(normalizer + coeffs, m, total_rows**0.5)
    rotation = below(rotation, n)
    ritz_matrix = nt(nn(rotation[:, :n], gram_stiff), rotation) * (1.0 / total_rows)
    return rotation, ritz_matrix


def pair_coefficients(rotation, basis):
    inner = jnp.where(lanes(16) >= 16, rotation, 0.0)
    both = jnp.concatenate([rotation, inner], axis=0)
    return nn(both[:, :48], basis)


def first_kernel(total_rows, sums_ref, coeffs_ref, ritz_ref):
    m = 16
    sums = sums_ref[...]
    gram_stiff = below(sums, 64)
    gram_mass = below(pltpu.roll(sums, 64, 1), 64)
    lane = lanes(m)
    start_mass = jnp.where((lane >= 64) & (lane < 80), sums[:m], 0.0)
    start = below(lower_solved(start_mass + diagonal(m, 0), m, total_rows**0.5), m)
    ritz_matrix = nt(nn(start[:, :m], gram_stiff[:m]), start) * (1.0 / total_rows)
    pulled = nn(ritz_matrix, start)
    residual = pltpu.roll(start, 16, 1) - pltpu.roll(pulled, 32, 1)
    basis = jnp.concatenate([start, residual, diagonal(m, 48)], axis=0)
    rotation, ritz_matrix = rayleigh_ritz(
        projected(basis, gram_stiff), projected(basis, gram_mass), total_rows
    )
    coeffs_ref[...] = pair_coefficients(rotation, basis)
    ritz_ref[...] = ritz_matrix


def last_kernel(total_rows, sums_ref, ritz_ref, coeffs_ref, out_ref):
    m = 16
    both = sums_ref[:128]
    turned = both.T
    row, lane = sublanes(128), lanes(128)
    stiff_diagonal = jnp.broadcast_to(sums_ref[128:129], (128, 128))
    gram_stiff = jnp.where(row > lane, both, jnp.where(row < lane, turned, stiff_diagonal))
    gram_mass = jnp.where(row > lane, turned, both)
    rotation, ritz_matrix = rayleigh_ritz(
        below(gram_stiff[:48], 48), below(gram_mass[:48], 48), total_rows
    )
    of_x = below(rotation, m)
    wide = nn(rotation[:, :m], jnp.concatenate([ritz_ref[...], jnp.zeros((m, 112), jnp.float32)], axis=1))
    pulled = nn(ritz_matrix, rotation)
    residual = (
        pltpu.roll(of_x, 16, 1) + pltpu.roll(rotation - of_x, 32, 1) + pltpu.roll(wide - pulled, 80, 1)
    )
    basis = jnp.concatenate([rotation, residual, rotation - of_x], axis=0)
    rotation, ritz_matrix = rayleigh_ritz(
        projected(basis, gram_stiff), projected(basis, gram_mass), total_rows
    )
    coeffs_ref[...] = pair_coefficients(rotation, basis)
    out_ref[...] = ritz_matrix


def coefficients(kernel, total_rows, *operands):
    return pl.pallas_call(
        functools.partial(kernel, total_rows),
        out_shape=(
            jax.ShapeDtypeStruct((32, 128), jnp.float32),
            jax.ShapeDtypeStruct((16, 16), jnp.float32),
        ),
        compiler_params=pltpu.CompilerParams(vmem_limit_bytes=16 * 1024 * 1024),
        name=kernel.__name__,
    )(*operands)


def packed(gram_stiff, gram_mass):
    size = gram_stiff.shape[0]
    low = jnp.tril(jnp.ones((size, size), bool), -1)
    both = jnp.where(low, gram_stiff, gram_mass)
    return jnp.concatenate([both, jnp.broadcast_to(jnp.diagonal(gram_stiff)[None], (8, size))])


def on_device(stiff_tiles, tile_mask, edge_star, start_modes, start_directions):
    m = start_modes.shape[0]
    total_rows = edge_star.shape[0] * lax.axis_size(SLAB)
    star = edge_star[None, :]
    fields = jnp.concatenate(
        [start_modes, start_directions, start_modes * star, jnp.broadcast_to(star, (8, star.shape[1]))]
    )
    fields = with_halo(fields)
    modes, directions, mass_modes = fields[:m], fields[m : 2 * m], fields[2 * m : 3 * m]
    star_ext = fields[3 * m : 3 * m + 1]
    applied = band(fields[: 3 * m], stiff_tiles, tile_mask)
    applied_modes = with_halo(applied[:m])
    twice = band(applied_modes, stiff_tiles, tile_mask)

    basis = jnp.concatenate([modes, applied_modes, mass_modes, directions])
    own = basis[:, TILE:-TILE]
    rest = jnp.concatenate([twice, applied[2 * m : 3 * m], applied[m : 2 * m]])
    applied_own = jnp.concatenate([applied[:m], rest])
    gram_stiff = gram(own, applied_own)
    gram_mass = gram(own, own * star)
    sums = slab_sum(jnp.concatenate([symmetric(gram_stiff), symmetric(gram_mass)], axis=1))
    applied_basis = jnp.concatenate([applied_modes, with_halo(rest)])
    coeffs, ritz_matrix = coefficients(first_kernel, total_rows, sums)

    coeffs = coeffs[:, : 4 * m]
    pair = product(coeffs, basis)
    applied_pair = product(coeffs, applied_basis)
    modes, directions = pair[:m], pair[m:]
    mass_modes = modes * star_ext
    residual = applied_pair[:m] - product(ritz_matrix, mass_modes)
    fields = jnp.concatenate(
        [residual, applied_pair[m:], mass_modes, residual * star_ext, directions * star_ext]
    )
    applied = band(fields, stiff_tiles, tile_mask)
    applied_residual = applied[:m]
    twice = band(with_halo(applied_residual), stiff_tiles, tile_mask)
    inner = slice(TILE, -TILE)
    own = jnp.concatenate(
        [
            modes[:, inner],
            residual[:, inner],
            directions[:, inner],
            applied_residual,
            fields[m:, inner],
        ]
    )
    applied_own = jnp.concatenate(
        [applied_pair[:m, inner], applied_residual, applied_pair[m:, inner], twice, applied[m:]]
    )
    gram_stiff = symmetric(gram(own, applied_own))
    gram_mass = symmetric(gram(own, own * star))
    sums = slab_sum(packed(gram_stiff, gram_mass))
    coeffs, ritz_matrix = coefficients(last_kernel, total_rows, sums, ritz_matrix)
    result = product(coeffs, own)
    return (result[:m], result[m:], ritz_matrix)


def solution(mesh):
    fine = Mesh(mesh.devices.reshape(-1, 4, 2, 4), ("z", "y", "core", "x"))
    in_specs = (
        P(SLAB, None, None, None),
        P(SLAB, None),
        P(SLAB),
        P(None, SLAB),
        P(None, SLAB),
    )
    out_specs = (P(None, SLAB), P(None, SLAB), P())
    return jax.shard_map(
        on_device, mesh=fine, in_specs=in_specs, out_specs=out_specs, check_vma=False
    )
```

```python
import functools

import jax
import jax.numpy as jnp
from jax import lax
from jax.experimental import pallas as pl
from jax.experimental.pallas import tpu as pltpu
from jax.sharding import Mesh
from jax.sharding import PartitionSpec as P

SLAB = ("z", "y", "core")
TILE = 128
STEP_BLOCKS = 4
STEP = STEP_BLOCKS * TILE
VMEM = 56 * 1024 * 1024
WIDTH = 4


def slab_sum(rows):
    parts = lax.axis_size(("y", "core"))
    shared = rows.reshape(parts, -1, 128)
    own = lax.all_to_all(shared, ("y", "core"), 0, 0, tiled=True).sum(0)
    copies = jnp.broadcast_to(own[None], (lax.axis_size("z"),) + own.shape)
    own = lax.all_to_all(copies, "z", 0, 0, tiled=True).sum(0)
    copies = jnp.broadcast_to(own[None], (parts,) + own.shape)
    return lax.all_to_all(copies, ("y", "core"), 0, 0, tiled=True).reshape(rows.shape)


def from_left(edge):
    count = lax.axis_size(SLAB)
    return lax.ppermute(edge, SLAB, [(i, i + 1) for i in range(count - 1)])


def from_right(edge):
    count = lax.axis_size(SLAB)
    return lax.ppermute(edge, SLAB, [(i + 1, i) for i in range(count - 1)])


def split(values):
    high = values.astype(jnp.bfloat16)
    low = (values - high.astype(jnp.float32)).astype(jnp.bfloat16)
    return high, low


def gram(left, right):
    return lax.dot_general(
        left,
        right,
        (((1,), (1,)), ((), ())),
        precision=lax.Precision.HIGHEST,
        preferred_element_type=jnp.float32,
    )


def nn(left, right):
    return jnp.dot(left, right, precision=lax.Precision.HIGHEST, preferred_element_type=jnp.float32)


def nt(left, right):
    return gram(left, right)


def lanes(rows):
    return lax.broadcasted_iota(jnp.int32, (rows, 128), 1)


def sublanes(rows):
    return lax.broadcasted_iota(jnp.int32, (rows, 128), 0)


def diagonal(rows, shift):
    return jnp.where(lanes(rows) == sublanes(rows) + shift, 1.0, 0.0).astype(jnp.float32)


def below(matrix, limit):
    return jnp.where(lanes(matrix.shape[0]) < limit, matrix, 0.0)


def pivots(groups, first, lane, width):
    columns = [
        [jnp.broadcast_to(g[:, lane + j : lane + j + 1], (8, 128)) for g in groups]
        for j in range(width)
    ]

    def spread(values, row):
        return jnp.broadcast_to(values[row // 8][row % 8 : row % 8 + 1], (8, 128))

    block = [[spread(columns[j], first + i) for j in range(width)] for i in range(width)]
    rows = [spread(groups, first + i) for i in range(width)]
    return columns, block, rows


def solved(block, rows):
    width = len(rows)
    block, rows = [list(r) for r in block], list(rows)
    for i in range(width):
        scale = 1.0 / block[i][i]
        block[i] = [v * scale for v in block[i]]
        rows[i] = rows[i] * scale
        for k in range(width):
            if k != i:
                factor = block[k][i]
                for j in range(i + 1, width):
                    block[k][j] = block[k][j] - factor * block[i][j]
                rows[k] = rows[k] - factor * rows[i]
    return rows


def inverse(matrix, size):
    matrix = matrix + diagonal(size, 64)
    groups = [matrix[8 * t : 8 * t + 8] for t in range(size // 8)]
    row = sublanes(8)
    for first in range(0, size, WIDTH):
        columns, block, rows = pivots(groups, first, first, WIDTH)
        rows = solved(block, rows)
        for t in range(size // 8):
            for j in range(WIDTH):
                groups[t] = groups[t] - columns[j][t] * rows[j]
            for j in range(WIDTH):
                if t == (first + j) // 8:
                    groups[t] = jnp.where(row == (first + j) % 8, rows[j], groups[t])
    return jnp.concatenate(groups, axis=0)


def lower_solved(matrix, size, scale):
    groups = [matrix[8 * t : 8 * t + 8] for t in range(size // 8)]
    row = sublanes(8)
    result = [jnp.zeros((8, 128), jnp.float32) for _ in groups]
    for first in range(0, size, WIDTH):
        columns, block, rows = pivots(groups, first, 64 + first, WIDTH)
        whole = solved(block, rows)
        for i in range(WIDTH):
            inverse_root = lax.rsqrt(block[i][i]) * scale
            t, at = (first + i) // 8, (first + i) % 8
            result[t] = jnp.where(row == at, rows[i] * inverse_root, result[t])
            if i + 1 < WIDTH:
                turn = 1.0 / block[i][i]
                for k in range(i + 1, WIDTH):
                    factor = block[k][i] * turn
                    block[k] = [a - factor * b for a, b in zip(block[k], block[i])]
                    rows[k] = rows[k] - factor * rows[i]
        for t in range(size // 8):
            if 8 * t + 7 >= first + WIDTH:
                for j in range(WIDTH):
                    groups[t] = groups[t] - columns[j][t] * whole[j]
    return jnp.concatenate(result, axis=0)


def projected(basis, matrix):
    tall = jnp.concatenate([basis, jnp.zeros((80, 128), jnp.float32)], axis=0)
    return nt(nn(basis[:, : matrix.shape[0]], matrix), tall)


def rayleigh_ritz(gram_stiff, gram_mass, total_rows):
    m, n = 16, 48
    inverted = inverse(gram_stiff + 1.0 * gram_mass, n)
    coeffs = below(pltpu.roll(nn(gram_mass[:m, :n], inverted), 64, 1), n)
    padded = jnp.concatenate(
        [jnp.zeros((64, 128), jnp.float32), coeffs, jnp.zeros((48, 128), jnp.float32)], axis=0
    )
    normalizer = nt(nn(coeffs[:, :n], gram_mass), padded)
    rotation = lower_solved(normalizer + coeffs, m, total_rows**0.5)
    rotation = below(rotation, n)
    ritz_matrix = nt(nn(rotation[:, :n], gram_stiff), rotation) * (1.0 / total_rows)
    return rotation, ritz_matrix


def pair_coefficients(rotation, basis):
    inner = jnp.where(lanes(16) >= 16, rotation, 0.0)
    both = jnp.concatenate([rotation, inner], axis=0)
    return nn(both[:, :48], basis)


def first_kernel(total_rows, sums_ref, coeffs_ref, ritz_ref):
    m = 16
    sums = sums_ref[...]
    gram_stiff = below(sums, 64)
    gram_mass = below(pltpu.roll(sums, 64, 1), 64)
    lane = lanes(m)
    start_mass = jnp.where((lane >= 64) & (lane < 80), sums[:m], 0.0)
    start = below(lower_solved(start_mass + diagonal(m, 0), m, total_rows**0.5), m)
    ritz_matrix = nt(nn(start[:, :m], gram_stiff[:m]), start) * (1.0 / total_rows)
    pulled = nn(ritz_matrix, start)
    residual = pltpu.roll(start, 16, 1) - pltpu.roll(pulled, 32, 1)
    basis = jnp.concatenate([start, residual, diagonal(m, 48)], axis=0)
    rotation, ritz_matrix = rayleigh_ritz(
        projected(basis, gram_stiff), projected(basis, gram_mass), total_rows
    )
    coeffs_ref[...] = pair_coefficients(rotation, basis)
    ritz_ref[...] = ritz_matrix


def nn3(left, right):
    count = left.shape[0]
    left_high, left_low = split(left)
    right_high, right_low = split(right)
    by_high = jnp.dot(
        jnp.concatenate([left_high, left_low], axis=0), right_high, preferred_element_type=jnp.float32
    )
    by_low = jnp.dot(left_high, right_low, preferred_element_type=jnp.float32)
    return by_high[:count] + by_high[count:] + by_low


def both_parts(values):
    return jnp.concatenate(split(values), axis=0)


def nt_parts(left, right):
    return lax.dot_general(left, right, (((1,), (1,)), ((), ())), preferred_element_type=jnp.float32)


def folded(term):
    rows, columns = term.shape[0] // 2, term.shape[1] // 2
    term = term[:, :columns] + term[:, columns:]
    return term[:rows] + term[rows:]


def weight(mask_ref, block, side):
    return mask_ref[block, side].astype(jnp.float32)


def full_rows(mask_ref, tiles_ref, k):
    block = pl.program_id(0) * STEP_BLOCKS + k
    return jnp.concatenate(
        [
            tiles_ref[k, 0] * weight(mask_ref, block, 0),
            tiles_ref[k, 1],
            tiles_ref[k, 2] * weight(mask_ref, block, 1),
        ],
        axis=1,
    )


def apply_blocks(mask_ref, tiles_ref, parts_ref, store):
    start = pl.multiple_of(pl.program_id(0) * STEP, TILE)
    window = parts_ref[:, pl.ds(start, STEP + 2 * TILE)]
    for k in range(STEP_BLOCKS):
        right = both_parts(full_rows(mask_ref, tiles_ref, k))
        store(k, folded(nt_parts(window[:, k * TILE : (k + 3) * TILE], right)))


def fill_parts(parts_ref, row, start, values):
    count, width = values.shape
    high, low = split(values)
    half = parts_ref.shape[0] // 2
    parts_ref[row : row + count, start : start + width] = high
    parts_ref[half + row : half + row + count, start : start + width] = low


def chunks(width):
    return [slice(c, c + STEP) for c in range(0, width, STEP)]


def edges_of(ref, step, low_ref, high_ref):
    @pl.when(step == 0)
    def _():
        high_ref[...] = ref[:, :TILE]

    @pl.when(step == pl.num_programs(0) - 1)
    def _():
        low_ref[...] = ref[:, STEP - TILE :]


def start_kernel(mask_ref, tiles_ref, x_ref, p_ref, star_ref, left_ref, right_ref, *rest):
    ax_ref, other_ref, ax_low, ax_high, parts_ref = rest
    step, width = pl.program_id(0), x_ref.shape[1]

    @pl.when(step == 0)
    def _():
        for start, ref in ((0, left_ref), (TILE + width, right_ref)):
            x, p, star = ref[:16], ref[16:32], ref[32:33]
            fill_parts(parts_ref, 0, start, jnp.concatenate([x, x * star, p], axis=0))
        for c in chunks(width):
            x, p = x_ref[:, c], p_ref[:, c]
            fields = jnp.concatenate([x, x * star_ref[:, c], p], axis=0)
            fill_parts(parts_ref, 0, TILE + c.start, fields)

    def store(k, term):
        at = slice(k * TILE, (k + 1) * TILE)
        ax_ref[:, at] = term[:16]
        other_ref[:, at] = term[16:]

    apply_blocks(mask_ref, tiles_ref, parts_ref, store)
    edges_of(ax_ref, step, ax_low, ax_high)


def gram_kernel(mask_ref, tiles_ref, x_ref, p_ref, star_ref, ax_ref, other_ref, *rest):
    left_ref, right_ref, twice_ref, sums_ref, low_ref, high_ref, parts_ref, total_ref, edge_ref = rest
    step, width = pl.program_id(0), ax_ref.shape[1]

    @pl.when(step == 0)
    def _():
        fill_parts(parts_ref, 0, 0, left_ref[...])
        fill_parts(parts_ref, 0, TILE + width, right_ref[...])
        for c in chunks(width):
            fill_parts(parts_ref, 0, TILE + c.start, ax_ref[:, c])
        total_ref[...] = jnp.zeros_like(total_ref)

    def store(k, term):
        twice_ref[:, k * TILE : (k + 1) * TILE] = term

    apply_blocks(mask_ref, tiles_ref, parts_ref, store)
    here = pl.ds(pl.multiple_of(step * STEP, TILE), STEP)
    x, p, star, ax, other = (r[:, here] for r in (x_ref, p_ref, star_ref, ax_ref, other_ref))
    basis = jnp.concatenate([x, ax, x * star, p], axis=0)
    applied = jnp.concatenate([ax, twice_ref[...], other, basis * star], axis=0)
    total_ref[...] += nt_parts(both_parts(basis), both_parts(applied))
    edge_ref[...] = jnp.concatenate([twice_ref[...], other], axis=0)
    edges_of(edge_ref, step, low_ref, high_ref)

    @pl.when(step == pl.num_programs(0) - 1)
    def _():
        sums = folded(total_ref[...])
        turned = jnp.concatenate([sums, jnp.zeros((64, 128), jnp.float32)], axis=0).T
        turned = jnp.where(lanes(64) < 64, turned[:64], pltpu.roll(turned[64:], 64, 1))
        sums_ref[...] = 0.5 * (sums + turned)


def middle_kernel(mask_ref, tiles_ref, coeffs_ref, ritz_ref, *rest):
    own_refs, left_refs, right_refs = rest[:6], rest[6:9], rest[9:12]
    out_ref, residual_ref, ax_ref, applied_ref, high_ref, parts_ref, all_ref = rest[12:]
    step, width = pl.program_id(0), own_refs[0].shape[1]

    def update(start, x, p, star, ax, twice, other):
        coeffs = coeffs_ref[:, :64]
        pair = nn3(coeffs, jnp.concatenate([x, ax, x * star, p], axis=0))
        applied = nn3(coeffs, jnp.concatenate([ax, twice, other], axis=0))
        x, p = pair[:16], pair[16:]
        mx = x * star
        r = applied[:16] - nn(ritz_ref[...], mx)
        fields = jnp.concatenate([r, applied[16:], mx, r * star, p * star], axis=0)
        fill_parts(parts_ref, 0, start, fields)
        if TILE <= start < TILE + width:
            here = slice(start - TILE, start - TILE + x.shape[1])
            all_ref[:, here] = jnp.concatenate([x, r, p, fields[16:], applied[:16]], axis=0)

    @pl.when(step == 0)
    def _():
        for start, refs in ((0, left_refs), (TILE + width, right_refs)):
            first, ax, last = (r[...] for r in refs)
            update(start, first[:16], first[16:32], first[32:33], ax, last[:16], last[16:])
        for c in chunks(width):
            update(TILE + c.start, *(r[:, c] for r in own_refs))

    def store(k, term):
        at = slice(k * TILE, (k + 1) * TILE)
        residual_ref[:, at] = term[:16]
        applied_ref[:, at] = term[16:]

    apply_blocks(mask_ref, tiles_ref, parts_ref, store)
    here = pl.ds(pl.multiple_of(step * STEP, TILE), STEP)
    out_ref[...] = all_ref[:112, here]
    ax_ref[...] = all_ref[112:, here]

    @pl.when(step == 0)
    def _():
        high_ref[...] = residual_ref[:, :TILE]


def pack_kernel(mask_ref, tiles_ref, star_ref, own_ref, ar_ref, ax_ref, applied_ref, right_ref, *rest):
    sums_ref, parts_ref, stiff_ref, mass_ref = rest
    step, width = pl.program_id(0), star_ref.shape[1]

    @pl.when(step == 0)
    def _():
        fill_parts(parts_ref, 0, width, right_ref[...])
        for c in chunks(width):
            fill_parts(parts_ref, 0, c.start, ar_ref[:, c])
        stiff_ref[...] = jnp.zeros_like(stiff_ref)
        mass_ref[...] = jnp.zeros_like(mass_ref)

    start = pl.multiple_of(step * STEP, TILE)
    window = parts_ref[:, pl.ds(start, STEP + TILE)]
    terms = []
    for k in range(STEP_BLOCKS):
        twofold = 2.0 * weight(mask_ref, step * STEP_BLOCKS + k, 1)
        row = jnp.concatenate([tiles_ref[k, 1], tiles_ref[k, 2] * twofold], axis=1)
        terms.append(folded(nt_parts(window[:, k * TILE : (k + 2) * TILE], both_parts(row))))
    twice = jnp.concatenate(terms, axis=1)
    here = pl.ds(start, STEP)
    own, ar, star = own_ref[:, here], ar_ref[:, here], star_ref[:, here]
    basis = jnp.concatenate([own, ar], axis=0)
    applied = jnp.concatenate(
        [ax_ref[:, here], ar, own[48:64], applied_ref[:, here], twice], axis=0
    )
    left = both_parts(basis)
    stiff_ref[...] += nt_parts(left, both_parts(applied))
    mass_ref[...] += nt_parts(left, both_parts(basis * star))

    @pl.when(step == pl.num_programs(0) - 1)
    def _():
        stiff, mass = folded(stiff_ref[...]), folded(mass_ref[...])
        row, lane = sublanes(128), lanes(128)
        stiff = jnp.where((row >= 112) & (lane >= 112), 0.5 * (stiff + stiff.T), stiff)
        sums_ref[:128] = jnp.where(row > lane, stiff, mass)
        along = jnp.sum(jnp.where(row == lane, stiff, 0.0), axis=0, keepdims=True)
        sums_ref[128:] = jnp.broadcast_to(along, (8, 128))


def last_kernel(total_rows, sums_ref, ritz_ref, own_ref, ar_ref, modes_ref, directions_ref, out_ref):
    m = 16
    both = sums_ref[:128]
    turned = both.T
    row, lane = sublanes(128), lanes(128)
    stiff_diagonal = jnp.broadcast_to(sums_ref[128:129], (128, 128))
    gram_stiff = jnp.where(row > lane, both, jnp.where(row < lane, turned, stiff_diagonal))
    gram_mass = jnp.where(row > lane, turned, both)
    rotation, ritz_matrix = rayleigh_ritz(
        below(gram_stiff[:48], 48), below(gram_mass[:48], 48), total_rows
    )
    of_x = below(rotation, m)
    of_r = below(rotation, 2 * m) - of_x
    of_p = rotation - of_x - of_r
    wide = nn(rotation[:, :m], jnp.concatenate([ritz_ref[...], jnp.zeros((m, 112), jnp.float32)], axis=1))
    pulled = nn(ritz_matrix, rotation)
    residual = (
        pltpu.roll(of_x, 16, 1)
        + pltpu.roll(of_r, 96, 1)
        + pltpu.roll(of_p, 16, 1)
        + pltpu.roll(wide - pulled, 64, 1)
    )
    basis = jnp.concatenate([rotation, residual, rotation - of_x], axis=0)
    rotation, ritz_matrix = rayleigh_ritz(
        projected(basis, gram_stiff), projected(basis, gram_mass), total_rows
    )
    out_ref[...] = ritz_matrix
    coeffs = pair_coefficients(rotation, basis)
    for c in chunks(own_ref.shape[1]):
        pair = nn3(coeffs, jnp.concatenate([own_ref[:, c], ar_ref[:, c]], axis=0))
        modes_ref[:, c] = pair[:m]
        directions_ref[:, c] = pair[m:]


def shape(*dims):
    return jax.ShapeDtypeStruct(dims, jnp.float32)


def params():
    return pltpu.CompilerParams(vmem_limit_bytes=VMEM)


def on_blocks(kernel, stepped, whole, scratch, mask, tiles, *operands):
    width = tiles.shape[0] * TILE
    return pl.pallas_call(
        kernel,
        grid=(tiles.shape[0] // STEP_BLOCKS,),
        in_specs=[
            pl.BlockSpec(memory_space=pltpu.SMEM),
            pl.BlockSpec((STEP_BLOCKS, 3, TILE, TILE), lambda i: (i, 0, 0, 0)),
        ]
        + [pl.BlockSpec(o.shape, lambda i: (0, 0)) for o in operands],
        out_specs=[pl.BlockSpec((r, STEP), lambda i: (0, i)) for r in stepped]
        + [pl.BlockSpec(w, lambda i: (0, 0)) for w in whole],
        out_shape=[shape(r, width) for r in stepped] + [shape(*w) for w in whole],
        scratch_shapes=scratch,
        compiler_params=params(),
        name=kernel.__name__,
    )(mask, tiles, *operands)


def on_device(stiff_tiles, tile_mask, edge_star, start_modes, start_directions):
    m, width = start_modes.shape
    total_rows = width * lax.axis_size(SLAB)
    star = edge_star[None, :]

    def edge(at):
        tail = jnp.broadcast_to(star[:, at], (8, TILE))
        return jnp.concatenate([start_modes[:, at], start_directions[:, at], tail])

    def parts(rows, halos):
        return pltpu.VMEM((2 * rows, width + halos * TILE), jnp.bfloat16)

    left = [from_left(edge(slice(width - TILE, width)))]
    right = [from_right(edge(slice(0, TILE)))]
    vectors = (start_modes, start_directions, star)
    applied, other, low, high = on_blocks(
        start_kernel, (m, 2 * m), ((m, TILE),) * 2, [parts(3 * m, 2)],
        tile_mask, stiff_tiles, *vectors, left[0], right[0],
    )
    left.append(from_left(low))
    right.append(from_right(high))
    twice, sums, low, high = on_blocks(
        gram_kernel, (m,), ((4 * m, 128), (3 * m, TILE), (3 * m, TILE)),
        [parts(m, 2), pltpu.VMEM((8 * m, 256), jnp.float32), pltpu.VMEM((3 * m, STEP), jnp.float32)],
        tile_mask, stiff_tiles, *vectors, applied, other, left[1], right[1],
    )
    left.append(from_left(low))
    right.append(from_right(high))
    sums = slab_sum(sums)
    coeffs, ritz_matrix = pl.pallas_call(
        functools.partial(first_kernel, total_rows),
        out_shape=(shape(2 * m, 128), shape(m, m)),
        compiler_params=params(),
        name="first_kernel",
    )(sums)
    own, applied_residual, applied, other, high = on_blocks(
        middle_kernel, (7 * m, m, m, 4 * m), ((m, TILE),),
        [parts(5 * m, 2), pltpu.VMEM((8 * m, width), jnp.float32)],
        tile_mask, stiff_tiles, coeffs, ritz_matrix, *vectors, applied, twice, other, *left, *right,
    )
    (sums,) = on_blocks(
        pack_kernel, (), ((8 * m + 8, 128),),
        [parts(m, 1)] + [pltpu.VMEM((16 * m, 256), jnp.float32)] * 2,
        tile_mask, stiff_tiles, star, own, applied_residual, applied, other, from_right(high),
    )
    sums = slab_sum(sums)
    return pl.pallas_call(
        functools.partial(last_kernel, total_rows),
        out_shape=(shape(m, width), shape(m, width), shape(m, m)),
        compiler_params=params(),
        name="last_kernel",
    )(sums, ritz_matrix, own, applied_residual)


def solution(mesh):
    fine = Mesh(mesh.devices.reshape(-1, 4, 2, 4), ("z", "y", "core", "x"))
    in_specs = (
        P(SLAB, None, None, None),
        P(SLAB, None),
        P(SLAB),
        P(None, SLAB),
        P(None, SLAB),
    )
    out_specs = (P(None, SLAB), P(None, SLAB), P())
    return jax.shard_map(
        on_device, mesh=fine, in_specs=in_specs, out_specs=out_specs, check_vma=False
    )
```

```python
import functools

import jax
import jax.numpy as jnp
from jax import lax
from jax.experimental import pallas as pl
from jax.experimental.pallas import tpu as pltpu
from jax.sharding import Mesh
from jax.sharding import PartitionSpec as P

SLAB = ("z", "y", "core")
TILE = 128
STEP_BLOCKS = 8
STEP = STEP_BLOCKS * TILE
VMEM = 20 * 1024 * 1024
WIDTH = 4


def slab_sum(rows):
    parts = lax.axis_size(("y", "core"))
    shared = rows.reshape(parts, -1, 128)
    own = lax.all_to_all(shared, ("y", "core"), 0, 0, tiled=True).sum(0)
    copies = jnp.broadcast_to(own[None], (lax.axis_size("z"),) + own.shape)
    own = lax.all_to_all(copies, "z", 0, 0, tiled=True).sum(0)
    copies = jnp.broadcast_to(own[None], (parts,) + own.shape)
    return lax.all_to_all(copies, ("y", "core"), 0, 0, tiled=True).reshape(rows.shape)


def from_left(edge):
    count = lax.axis_size(SLAB)
    return lax.ppermute(edge, SLAB, [(i, i + 1) for i in range(count - 1)])


def from_right(edge):
    count = lax.axis_size(SLAB)
    return lax.ppermute(edge, SLAB, [(i + 1, i) for i in range(count - 1)])


def split(values):
    high = values.astype(jnp.bfloat16)
    low = (values - high.astype(jnp.float32)).astype(jnp.bfloat16)
    return high, low


def gram(left, right):
    return lax.dot_general(
        left,
        right,
        (((1,), (1,)), ((), ())),
        precision=lax.Precision.HIGHEST,
        preferred_element_type=jnp.float32,
    )


def nn(left, right):
    return jnp.dot(left, right, precision=lax.Precision.HIGHEST, preferred_element_type=jnp.float32)


def nt(left, right):
    return gram(left, right)


def lanes(rows):
    return lax.broadcasted_iota(jnp.int32, (rows, 128), 1)


def sublanes(rows):
    return lax.broadcasted_iota(jnp.int32, (rows, 128), 0)


def diagonal(rows, shift):
    return jnp.where(lanes(rows) == sublanes(rows) + shift, 1.0, 0.0).astype(jnp.float32)


def below(matrix, limit):
    return jnp.where(lanes(matrix.shape[0]) < limit, matrix, 0.0)


def pivots(groups, first, lane, width):
    columns = [
        [jnp.broadcast_to(g[:, lane + j : lane + j + 1], (8, 128)) for g in groups]
        for j in range(width)
    ]

    def spread(values, row):
        return jnp.broadcast_to(values[row // 8][row % 8 : row % 8 + 1], (8, 128))

    block = [[spread(columns[j], first + i) for j in range(width)] for i in range(width)]
    rows = [spread(groups, first + i) for i in range(width)]
    return columns, block, rows


def solved(block, rows):
    width = len(rows)
    block, rows = [list(r) for r in block], list(rows)
    for i in range(width):
        scale = 1.0 / block[i][i]
        block[i] = [v * scale for v in block[i]]
        rows[i] = rows[i] * scale
        for k in range(width):
            if k != i:
                factor = block[k][i]
                for j in range(i + 1, width):
                    block[k][j] = block[k][j] - factor * block[i][j]
                rows[k] = rows[k] - factor * rows[i]
    return rows


def inverse(matrix, size):
    matrix = matrix + diagonal(size, 64)
    groups = [matrix[8 * t : 8 * t + 8] for t in range(size // 8)]
    row = sublanes(8)
    for first in range(0, size, WIDTH):
        columns, block, rows = pivots(groups, first, first, WIDTH)
        rows = solved(block, rows)
        for t in range(size // 8):
            for j in range(WIDTH):
                groups[t] = groups[t] - columns[j][t] * rows[j]
            for j in range(WIDTH):
                if t == (first + j) // 8:
                    groups[t] = jnp.where(row == (first + j) % 8, rows[j], groups[t])
    return jnp.concatenate(groups, axis=0)


def lower_solved(matrix, size, scale):
    groups = [matrix[8 * t : 8 * t + 8] for t in range(size // 8)]
    row = sublanes(8)
    result = [jnp.zeros((8, 128), jnp.float32) for _ in groups]
    for first in range(0, size, WIDTH):
        columns, block, rows = pivots(groups, first, 64 + first, WIDTH)
        whole = solved(block, rows)
        for i in range(WIDTH):
            inverse_root = lax.rsqrt(block[i][i]) * scale
            t, at = (first + i) // 8, (first + i) % 8
            result[t] = jnp.where(row == at, rows[i] * inverse_root, result[t])
            if i + 1 < WIDTH:
                turn = 1.0 / block[i][i]
                for k in range(i + 1, WIDTH):
                    factor = block[k][i] * turn
                    block[k] = [a - factor * b for a, b in zip(block[k], block[i])]
                    rows[k] = rows[k] - factor * rows[i]
        for t in range(size // 8):
            if 8 * t + 7 >= first + WIDTH:
                for j in range(WIDTH):
                    groups[t] = groups[t] - columns[j][t] * whole[j]
    return jnp.concatenate(result, axis=0)


def projected(basis, matrix):
    tall = jnp.concatenate([basis, jnp.zeros((80, 128), jnp.float32)], axis=0)
    return nt(nn(basis[:, : matrix.shape[0]], matrix), tall)


def rayleigh_ritz(gram_stiff, gram_mass, total_rows):
    m, n = 16, 48
    inverted = inverse(gram_stiff + 1.0 * gram_mass, n)
    coeffs = below(pltpu.roll(nn(gram_mass[:m, :n], inverted), 64, 1), n)
    padded = jnp.concatenate(
        [jnp.zeros((64, 128), jnp.float32), coeffs, jnp.zeros((48, 128), jnp.float32)], axis=0
    )
    normalizer = nt(nn(coeffs[:, :n], gram_mass), padded)
    rotation = lower_solved(normalizer + coeffs, m, total_rows**0.5)
    rotation = below(rotation, n)
    ritz_matrix = nt(nn(rotation[:, :n], gram_stiff), rotation) * (1.0 / total_rows)
    return rotation, ritz_matrix


def pair_coefficients(rotation, basis):
    inner = jnp.where(lanes(16) >= 16, rotation, 0.0)
    both = jnp.concatenate([rotation, inner], axis=0)
    return nn(both[:, :48], basis)


def first_kernel(total_rows, sums_ref, coeffs_ref, ritz_ref):
    m = 16
    sums = sums_ref[...]
    gram_stiff = below(sums, 64)
    gram_mass = below(pltpu.roll(sums, 64, 1), 64)
    lane = lanes(m)
    start_mass = jnp.where((lane >= 64) & (lane < 80), sums[:m], 0.0)
    start = below(lower_solved(start_mass + diagonal(m, 0), m, total_rows**0.5), m)
    ritz_matrix = nt(nn(start[:, :m], gram_stiff[:m]), start) * (1.0 / total_rows)
    pulled = nn(ritz_matrix, start)
    residual = pltpu.roll(start, 16, 1) - pltpu.roll(pulled, 32, 1)
    basis = jnp.concatenate([start, residual, diagonal(m, 48)], axis=0)
    rotation, ritz_matrix = rayleigh_ritz(
        projected(basis, gram_stiff), projected(basis, gram_mass), total_rows
    )
    coeffs_ref[...] = pair_coefficients(rotation, basis)
    ritz_ref[...] = ritz_matrix


def nn3(left, right):
    count = left.shape[0]
    left_high, left_low = split(left)
    right_high, right_low = split(right)
    by_high = jnp.dot(
        jnp.concatenate([left_high, left_low], axis=0), right_high, preferred_element_type=jnp.float32
    )
    by_low = jnp.dot(left_high, right_low, preferred_element_type=jnp.float32)
    return by_high[:count] + by_high[count:] + by_low


def both_parts(values):
    return jnp.concatenate(split(values), axis=0)


def nt_parts(left, right):
    return lax.dot_general(left, right, (((1,), (1,)), ((), ())), preferred_element_type=jnp.float32)


def folded(term):
    rows, columns = term.shape[0] // 2, term.shape[1] // 2
    term = term[:, :columns] + term[:, columns:]
    return term[:rows] + term[rows:]


def weight(mask_ref, block, side):
    return mask_ref[block, side].astype(jnp.float32)


def full_rows(mask_ref, tiles_ref, k):
    block = pl.program_id(0) * STEP_BLOCKS + k
    return jnp.concatenate(
        [
            tiles_ref[k, 0] * weight(mask_ref, block, 0),
            tiles_ref[k, 1],
            tiles_ref[k, 2] * weight(mask_ref, block, 1),
        ],
        axis=1,
    )


def apply_blocks(mask_ref, tiles_ref, parts_ref, store):
    start = pl.multiple_of(pl.program_id(0) * STEP, TILE)
    window = parts_ref[:, pl.ds(start, STEP + 2 * TILE)]
    for k in range(STEP_BLOCKS):
        right = both_parts(full_rows(mask_ref, tiles_ref, k))
        store(k, folded(nt_parts(window[:, k * TILE : (k + 3) * TILE], right)))


def fill_parts(parts_ref, row, start, values):
    count, width = values.shape
    high, low = split(values)
    half = parts_ref.shape[0] // 2
    parts_ref[row : row + count, start : start + width] = high
    parts_ref[half + row : half + row + count, start : start + width] = low


def chunks(width):
    return [slice(c, c + STEP) for c in range(0, width, STEP)]


def edges_of(ref, step, low_ref, high_ref):
    @pl.when(step == 0)
    def _():
        high_ref[...] = ref[:, :TILE]

    @pl.when(step == pl.num_programs(0) - 1)
    def _():
        low_ref[...] = ref[:, STEP - TILE :]


def start_kernel(mask_ref, tiles_ref, x_ref, p_ref, star_ref, left_ref, right_ref, *rest):
    ax_ref, other_ref, ax_low, ax_high, parts_ref = rest
    step, width = pl.program_id(0), x_ref.shape[1]

    @pl.when(step == 0)
    def _():
        for start, ref in ((0, left_ref), (TILE + width, right_ref)):
            x, p, star = ref[:16], ref[16:32], ref[32:33]
            fill_parts(parts_ref, 0, start, jnp.concatenate([x, x * star, p], axis=0))
        for c in chunks(width):
            x, p = x_ref[:, c], p_ref[:, c]
            fields = jnp.concatenate([x, x * star_ref[:, c], p], axis=0)
            fill_parts(parts_ref, 0, TILE + c.start, fields)

    def store(k, term):
        at = slice(k * TILE, (k + 1) * TILE)
        ax_ref[:, at] = term[:16]
        other_ref[:, at] = term[16:]

    apply_blocks(mask_ref, tiles_ref, parts_ref, store)
    edges_of(ax_ref, step, ax_low, ax_high)


def gram_kernel(mask_ref, tiles_ref, x_ref, p_ref, star_ref, ax_ref, other_ref, *rest):
    left_ref, right_ref, twice_ref, sums_ref, low_ref, high_ref, parts_ref, total_ref, edge_ref = rest
    step, width = pl.program_id(0), ax_ref.shape[1]

    @pl.when(step == 0)
    def _():
        fill_parts(parts_ref, 0, 0, left_ref[...])
        fill_parts(parts_ref, 0, TILE + width, right_ref[...])
        for c in chunks(width):
            fill_parts(parts_ref, 0, TILE + c.start, ax_ref[:, c])
        total_ref[...] = jnp.zeros_like(total_ref)

    def store(k, term):
        twice_ref[:, k * TILE : (k + 1) * TILE] = term

    apply_blocks(mask_ref, tiles_ref, parts_ref, store)
    here = pl.ds(pl.multiple_of(step * STEP, TILE), STEP)
    x, p, star, ax, other = (r[:, here] for r in (x_ref, p_ref, star_ref, ax_ref, other_ref))
    basis = jnp.concatenate([x, ax, x * star, p], axis=0)
    applied = jnp.concatenate([ax, twice_ref[...], other, basis * star], axis=0)
    total_ref[...] += nt_parts(both_parts(basis), both_parts(applied))
    edge_ref[...] = jnp.concatenate([twice_ref[...], other], axis=0)
    edges_of(edge_ref, step, low_ref, high_ref)

    @pl.when(step == pl.num_programs(0) - 1)
    def _():
        sums = folded(total_ref[...])
        turned = jnp.concatenate([sums, jnp.zeros((64, 128), jnp.float32)], axis=0).T
        turned = jnp.where(lanes(64) < 64, turned[:64], pltpu.roll(turned[64:], 64, 1))
        sums_ref[...] = 0.5 * (sums + turned)


def middle_kernel(mask_ref, tiles_ref, coeffs_ref, ritz_ref, *rest):
    own_refs, left_refs, right_refs = rest[:6], rest[6:9], rest[9:12]
    out_ref, residual_ref, ax_ref, applied_ref, high_ref, parts_ref, all_ref = rest[12:]
    step, width = pl.program_id(0), own_refs[0].shape[1]

    def update(start, x, p, star, ax, twice, other):
        coeffs = coeffs_ref[:, :64]
        pair = nn3(coeffs, jnp.concatenate([x, ax, x * star, p], axis=0))
        applied = nn3(coeffs, jnp.concatenate([ax, twice, other], axis=0))
        x, p = pair[:16], pair[16:]
        mx = x * star
        r = applied[:16] - nn(ritz_ref[...], mx)
        fields = jnp.concatenate([r, applied[16:], mx, r * star, p * star], axis=0)
        fill_parts(parts_ref, 0, start, fields)
        if TILE <= start < TILE + width:
            here = slice(start - TILE, start - TILE + x.shape[1])
            all_ref[:, here] = jnp.concatenate([x, r, p, fields[16:], applied[:16]], axis=0)

    @pl.when(step == 0)
    def _():
        for start, refs in ((0, left_refs), (TILE + width, right_refs)):
            first, ax, last = (r[...] for r in refs)
            update(start, first[:16], first[16:32], first[32:33], ax, last[:16], last[16:])
        for c in chunks(width):
            update(TILE + c.start, *(r[:, c] for r in own_refs))

    def store(k, term):
        at = slice(k * TILE, (k + 1) * TILE)
        residual_ref[:, at] = term[:16]
        applied_ref[:, at] = term[16:]

    apply_blocks(mask_ref, tiles_ref, parts_ref, store)
    here = pl.ds(pl.multiple_of(step * STEP, TILE), STEP)
    out_ref[...] = all_ref[:112, here]
    ax_ref[...] = all_ref[112:, here]

    @pl.when(step == 0)
    def _():
        high_ref[...] = residual_ref[:, :TILE]


def pack_kernel(mask_ref, tiles_ref, star_ref, own_ref, ar_ref, ax_ref, applied_ref, right_ref, *rest):
    sums_ref, parts_ref, stiff_ref, mass_ref = rest
    step, width = pl.program_id(0), star_ref.shape[1]

    @pl.when(step == 0)
    def _():
        fill_parts(parts_ref, 0, width, right_ref[...])
        for c in chunks(width):
            fill_parts(parts_ref, 0, c.start, ar_ref[:, c])
        stiff_ref[...] = jnp.zeros_like(stiff_ref)
        mass_ref[...] = jnp.zeros_like(mass_ref)

    start = pl.multiple_of(step * STEP, TILE)
    window = parts_ref[:, pl.ds(start, STEP + TILE)]
    terms = []
    for k in range(STEP_BLOCKS):
        twofold = 2.0 * weight(mask_ref, step * STEP_BLOCKS + k, 1)
        row = jnp.concatenate([tiles_ref[k, 1], tiles_ref[k, 2] * twofold], axis=1)
        terms.append(folded(nt_parts(window[:, k * TILE : (k + 2) * TILE], both_parts(row))))
    twice = jnp.concatenate(terms, axis=1)
    here = pl.ds(start, STEP)
    own, ar, star = own_ref[:, here], ar_ref[:, here], star_ref[:, here]
    basis = jnp.concatenate([own, ar], axis=0)
    applied = jnp.concatenate(
        [ax_ref[:, here], ar, own[48:64], applied_ref[:, here], twice], axis=0
    )
    left = both_parts(basis)
    stiff_ref[...] += nt_parts(left, both_parts(applied))
    mass_ref[...] += nt_parts(left, both_parts(basis * star))

    @pl.when(step == pl.num_programs(0) - 1)
    def _():
        stiff, mass = folded(stiff_ref[...]), folded(mass_ref[...])
        row, lane = sublanes(128), lanes(128)
        stiff = jnp.where((row >= 112) & (lane >= 112), 0.5 * (stiff + stiff.T), stiff)
        sums_ref[...] = jnp.where(row > lane, stiff, mass)
        along = jnp.sum(jnp.where(row == lane, stiff, 0.0), axis=1, keepdims=True)
        placed = nn(of_groups(8, 128), jnp.where(lane == 64 + row % 16, along, 0.0))
        taken = lanes(8)
        taken = (taken >= 64) & (taken < 80)
        sums_ref[16:24] = jnp.where(taken, placed, sums_ref[16:24])


def of_groups(groups, size):
    row = lax.broadcasted_iota(jnp.int32, (groups, size), 0)
    column = lax.broadcasted_iota(jnp.int32, (groups, size), 1)
    return jnp.where(column // 16 == row, 1.0, 0.0).astype(jnp.float32)


def last_kernel(total_rows, sums_ref, ritz_ref, own_ref, ar_ref, modes_ref, directions_ref, out_ref):
    m = 16
    both = sums_ref[...]
    turned = both.T
    row, lane = sublanes(128), lanes(128)
    group = lax.broadcasted_iota(jnp.int32, (128, 8), 0) // 16
    member = lax.broadcasted_iota(jnp.int32, (128, 8), 1)
    spread = nn(jnp.where(group == member, 1.0, 0.0).astype(jnp.float32), both[16:24])
    along = jnp.sum(jnp.where(lane == 64 + row % 16, spread, 0.0), axis=1, keepdims=True)
    gram_stiff = jnp.where(row > lane, both, jnp.where(row < lane, turned, along))
    gram_mass = jnp.where(row > lane, turned, both)
    of_r = jnp.where((lanes(m) >= 64) & (lanes(m) < 80), pltpu.roll(gram_mass[80:96], 64, 1), gram_mass[16:32])
    of_mx = jnp.where((lanes(m) >= 16) & (lanes(m) < 32), pltpu.roll(gram_mass[:16], 64, 1), gram_mass[64:80])
    gram_mass = jnp.concatenate(
        [gram_mass[:16], of_r, gram_mass[32:64], of_mx, gram_mass[80:]], axis=0
    )
    rotation, ritz_matrix = rayleigh_ritz(
        below(gram_stiff[:48], 48), below(gram_mass[:48], 48), total_rows
    )
    of_x = below(rotation, m)
    of_r = below(rotation, 2 * m) - of_x
    of_p = rotation - of_x - of_r
    wide = nn(rotation[:, :m], jnp.concatenate([ritz_ref[...], jnp.zeros((m, 112), jnp.float32)], axis=1))
    pulled = nn(ritz_matrix, rotation)
    residual = (
        pltpu.roll(of_x, 16, 1)
        + pltpu.roll(of_r, 96, 1)
        + pltpu.roll(of_p, 16, 1)
        + pltpu.roll(wide - pulled, 64, 1)
    )
    basis = jnp.concatenate([rotation, residual, rotation - of_x], axis=0)
    rotation, ritz_matrix = rayleigh_ritz(
        projected(basis, gram_stiff), projected(basis, gram_mass), total_rows
    )
    out_ref[...] = ritz_matrix
    coeffs = pair_coefficients(rotation, basis)
    for c in chunks(own_ref.shape[1]):
        pair = nn3(coeffs, jnp.concatenate([own_ref[:, c], ar_ref[:, c]], axis=0))
        modes_ref[:, c] = pair[:m]
        directions_ref[:, c] = pair[m:]


def shape(*dims):
    return jax.ShapeDtypeStruct(dims, jnp.float32)


def params():
    return pltpu.CompilerParams(vmem_limit_bytes=VMEM)


def on_blocks(kernel, stepped, whole, scratch, mask, tiles, *operands):
    width = tiles.shape[0] * TILE
    return pl.pallas_call(
        kernel,
        grid=(tiles.shape[0] // STEP_BLOCKS,),
        in_specs=[
            pl.BlockSpec(memory_space=pltpu.SMEM),
            pl.BlockSpec((STEP_BLOCKS, 3, TILE, TILE), lambda i: (i, 0, 0, 0)),
        ]
        + [pl.BlockSpec(o.shape, lambda i: (0, 0)) for o in operands],
        out_specs=[pl.BlockSpec((r, STEP), lambda i: (0, i)) for r in stepped]
        + [pl.BlockSpec(w, lambda i: (0, 0)) for w in whole],
        out_shape=[shape(r, width) for r in stepped] + [shape(*w) for w in whole],
        scratch_shapes=scratch,
        compiler_params=params(),
        name=kernel.__name__,
    )(mask, tiles, *operands)


def on_device(stiff_tiles, tile_mask, edge_star, start_modes, start_directions):
    m, width = start_modes.shape
    total_rows = width * lax.axis_size(SLAB)
    star = edge_star[None, :]

    def edge(at):
        tail = jnp.broadcast_to(star[:, at], (8, TILE))
        return jnp.concatenate([start_modes[:, at], start_directions[:, at], tail])

    def parts(rows, halos):
        return pltpu.VMEM((2 * rows, width + halos * TILE), jnp.bfloat16)

    left = [from_left(edge(slice(width - TILE, width)))]
    right = [from_right(edge(slice(0, TILE)))]
    vectors = (start_modes, start_directions, star)
    applied, other, low, high = on_blocks(
        start_kernel, (m, 2 * m), ((m, TILE),) * 2, [parts(3 * m, 2)],
        tile_mask, stiff_tiles, *vectors, left[0], right[0],
    )
    left.append(from_left(low))
    right.append(from_right(high))
    twice, sums, low, high = on_blocks(
        gram_kernel, (m,), ((4 * m, 128), (3 * m, TILE), (3 * m, TILE)),
        [parts(m, 2), pltpu.VMEM((8 * m, 256), jnp.float32), pltpu.VMEM((3 * m, STEP), jnp.float32)],
        tile_mask, stiff_tiles, *vectors, applied, other, left[1], right[1],
    )
    left.append(from_left(low))
    right.append(from_right(high))
    sums = slab_sum(sums)
    coeffs, ritz_matrix = pl.pallas_call(
        functools.partial(first_kernel, total_rows),
        out_shape=(shape(2 * m, 128), shape(m, m)),
        compiler_params=params(),
        name="first_kernel",
    )(sums)
    own, applied_residual, applied, other, high = on_blocks(
        middle_kernel, (7 * m, m, m, 4 * m), ((m, TILE),),
        [parts(5 * m, 2), pltpu.VMEM((8 * m, width), jnp.float32)],
        tile_mask, stiff_tiles, coeffs, ritz_matrix, *vectors, applied, twice, other, *left, *right,
    )
    (sums,) = on_blocks(
        pack_kernel, (), ((8 * m, 128),),
        [parts(m, 1)] + [pltpu.VMEM((16 * m, 256), jnp.float32)] * 2,
        tile_mask, stiff_tiles, star, own, applied_residual, applied, other, from_right(high),
    )
    sums = slab_sum(sums)
    return pl.pallas_call(
        functools.partial(last_kernel, total_rows),
        out_shape=(shape(m, width), shape(m, width), shape(m, m)),
        compiler_params=params(),
        name="last_kernel",
    )(sums, ritz_matrix, own, applied_residual)


def solution(mesh):
    fine = Mesh(mesh.devices.reshape(-1, 4, 2, 4), ("z", "y", "core", "x"))
    in_specs = (
        P(SLAB, None, None, None),
        P(SLAB, None),
        P(SLAB),
        P(None, SLAB),
        P(None, SLAB),
    )
    out_specs = (P(None, SLAB), P(None, SLAB), P())
    return jax.shard_map(
        on_device, mesh=fine, in_specs=in_specs, out_specs=out_specs, check_vma=False
    )
```

```python
import functools

import jax
import jax.numpy as jnp
from jax import lax
from jax.experimental import pallas as pl
from jax.experimental.pallas import tpu as pltpu
from jax.sharding import Mesh
from jax.sharding import PartitionSpec as P

SLAB = ("z", "y", "core")
TILE = 128
STEP_BLOCKS = 8
STEP = STEP_BLOCKS * TILE
VMEM = 20 * 1024 * 1024
WIDTH = 8


def slab_sum(rows):
    parts = lax.axis_size(("y", "core"))
    shared = rows.reshape(parts, -1, 128)
    own = lax.all_to_all(shared, ("y", "core"), 0, 0, tiled=True).sum(0)
    copies = jnp.broadcast_to(own[None], (lax.axis_size("z"),) + own.shape)
    own = lax.all_to_all(copies, "z", 0, 0, tiled=True).sum(0)
    copies = jnp.broadcast_to(own[None], (parts,) + own.shape)
    return lax.all_to_all(copies, ("y", "core"), 0, 0, tiled=True).reshape(rows.shape)


def from_left(edge):
    count = lax.axis_size(SLAB)
    return lax.ppermute(edge, SLAB, [(i, i + 1) for i in range(count - 1)])


def from_right(edge):
    count = lax.axis_size(SLAB)
    return lax.ppermute(edge, SLAB, [(i + 1, i) for i in range(count - 1)])


def split(values):
    high = values.astype(jnp.bfloat16)
    low = (values - high.astype(jnp.float32)).astype(jnp.bfloat16)
    return high, low


def gram(left, right):
    return lax.dot_general(
        left,
        right,
        (((1,), (1,)), ((), ())),
        precision=lax.Precision.HIGHEST,
        preferred_element_type=jnp.float32,
    )


def nn(left, right):
    return jnp.dot(left, right, precision=lax.Precision.HIGHEST, preferred_element_type=jnp.float32)


def nt(left, right):
    return gram(left, right)


def lanes(rows):
    return lax.broadcasted_iota(jnp.int32, (rows, 128), 1)


def sublanes(rows):
    return lax.broadcasted_iota(jnp.int32, (rows, 128), 0)


def diagonal(rows, shift):
    return jnp.where(lanes(rows) == sublanes(rows) + shift, 1.0, 0.0).astype(jnp.float32)


def below(matrix, limit):
    return jnp.where(lanes(matrix.shape[0]) < limit, matrix, 0.0)


def pivots(groups, first, lane, width):
    columns = [
        [jnp.broadcast_to(g[:, lane + j : lane + j + 1], (8, 128)) for g in groups]
        for j in range(width)
    ]

    def spread(values, row):
        return jnp.broadcast_to(values[row // 8][row % 8 : row % 8 + 1], (8, 128))

    block = [[spread(columns[j], first + i) for j in range(width)] for i in range(width)]
    rows = [spread(groups, first + i) for i in range(width)]
    return columns, block, rows


def solved(block, rows):
    width = len(rows)
    block, rows = [list(r) for r in block], list(rows)
    for i in range(width):
        scale = 1.0 / block[i][i]
        block[i] = [v * scale for v in block[i]]
        rows[i] = rows[i] * scale
        for k in range(width):
            if k != i:
                factor = block[k][i]
                for j in range(i + 1, width):
                    block[k][j] = block[k][j] - factor * block[i][j]
                rows[k] = rows[k] - factor * rows[i]
    return rows


def inverse(matrix, size):
    matrix = matrix + diagonal(size, 64)
    groups = [matrix[8 * t : 8 * t + 8] for t in range(size // 8)]
    row = sublanes(8)
    for first in range(0, size, WIDTH):
        columns, block, rows = pivots(groups, first, first, WIDTH)
        rows = solved(block, rows)
        for t in range(size // 8):
            for j in range(WIDTH):
                groups[t] = groups[t] - columns[j][t] * rows[j]
            for j in range(WIDTH):
                if t == (first + j) // 8:
                    groups[t] = jnp.where(row == (first + j) % 8, rows[j], groups[t])
    return jnp.concatenate(groups, axis=0)


def lower_solved(matrix, size, scale):
    groups = [matrix[8 * t : 8 * t + 8] for t in range(size // 8)]
    row = sublanes(8)
    result = [jnp.zeros((8, 128), jnp.float32) for _ in groups]
    for first in range(0, size, WIDTH):
        columns, block, rows = pivots(groups, first, 64 + first, WIDTH)
        whole = solved(block, rows)
        for i in range(WIDTH):
            inverse_root = lax.rsqrt(block[i][i]) * scale
            t, at = (first + i) // 8, (first + i) % 8
            result[t] = jnp.where(row == at, rows[i] * inverse_root, result[t])
            if i + 1 < WIDTH:
                turn = 1.0 / block[i][i]
                for k in range(i + 1, WIDTH):
                    factor = block[k][i] * turn
                    block[k] = [a - factor * b for a, b in zip(block[k], block[i])]
                    rows[k] = rows[k] - factor * rows[i]
        for t in range(size // 8):
            if 8 * t + 7 >= first + WIDTH:
                for j in range(WIDTH):
                    groups[t] = groups[t] - columns[j][t] * whole[j]
    return jnp.concatenate(result, axis=0)


def projected(basis, matrix):
    tall = jnp.concatenate([basis, jnp.zeros((80, 128), jnp.float32)], axis=0)
    return nt(nn(basis[:, : matrix.shape[0]], matrix), tall)


def rayleigh_ritz(gram_stiff, gram_mass, total_rows):
    m, n = 16, 48
    inverted = inverse(gram_stiff + 1.0 * gram_mass, n)
    coeffs = below(pltpu.roll(nn(gram_mass[:m, :n], inverted), 64, 1), n)
    padded = jnp.concatenate(
        [jnp.zeros((64, 128), jnp.float32), coeffs, jnp.zeros((48, 128), jnp.float32)], axis=0
    )
    normalizer = nt(nn(coeffs[:, :n], gram_mass), padded)
    rotation = lower_solved(normalizer + coeffs, m, total_rows**0.5)
    rotation = below(rotation, n)
    ritz_matrix = nt(nn(rotation[:, :n], gram_stiff), rotation) * (1.0 / total_rows)
    return rotation, ritz_matrix


def pair_coefficients(rotation, basis):
    inner = jnp.where(lanes(16) >= 16, rotation, 0.0)
    both = jnp.concatenate([rotation, inner], axis=0)
    return nn(both[:, :48], basis)


def first_kernel(total_rows, sums_ref, coeffs_ref, ritz_ref):
    m = 16
    sums = sums_ref[...]
    gram_stiff = below(sums, 64)
    gram_mass = below(pltpu.roll(sums, 64, 1), 64)
    lane = lanes(m)
    start_mass = jnp.where((lane >= 64) & (lane < 80), sums[:m], 0.0)
    start = below(lower_solved(start_mass + diagonal(m, 0), m, total_rows**0.5), m)
    ritz_matrix = nt(nn(start[:, :m], gram_stiff[:m]), start) * (1.0 / total_rows)
    pulled = nn(ritz_matrix, start)
    residual = pltpu.roll(start, 16, 1) - pltpu.roll(pulled, 32, 1)
    basis = jnp.concatenate([start, residual, diagonal(m, 48)], axis=0)
    rotation, ritz_matrix = rayleigh_ritz(
        projected(basis, gram_stiff), projected(basis, gram_mass), total_rows
    )
    coeffs_ref[...] = pair_coefficients(rotation, basis)
    ritz_ref[...] = ritz_matrix


def nn3(left, right):
    count = left.shape[0]
    left_high, left_low = split(left)
    right_high, right_low = split(right)
    by_high = jnp.dot(
        jnp.concatenate([left_high, left_low], axis=0), right_high, preferred_element_type=jnp.float32
    )
    by_low = jnp.dot(left_high, right_low, preferred_element_type=jnp.float32)
    return by_high[:count] + by_high[count:] + by_low


def both_parts(values):
    return jnp.concatenate(split(values), axis=0)


def nt_parts(left, right):
    return lax.dot_general(left, right, (((1,), (1,)), ((), ())), preferred_element_type=jnp.float32)


def folded(term):
    rows, columns = term.shape[0] // 2, term.shape[1] // 2
    term = term[:, :columns] + term[:, columns:]
    return term[:rows] + term[rows:]


def weight(mask_ref, block, side):
    return mask_ref[block, side].astype(jnp.float32)


def full_rows(mask_ref, tiles_ref, k):
    block = pl.program_id(0) * STEP_BLOCKS + k
    return jnp.concatenate(
        [
            tiles_ref[k, 0] * weight(mask_ref, block, 0),
            tiles_ref[k, 1],
            tiles_ref[k, 2] * weight(mask_ref, block, 1),
        ],
        axis=1,
    )


def apply_blocks(mask_ref, tiles_ref, parts_ref, store):
    start = pl.multiple_of(pl.program_id(0) * STEP, TILE)
    window = parts_ref[:, pl.ds(start, STEP + 2 * TILE)]
    for k in range(STEP_BLOCKS):
        right = both_parts(full_rows(mask_ref, tiles_ref, k))
        store(k, folded(nt_parts(window[:, k * TILE : (k + 3) * TILE], right)))


def fill_parts(parts_ref, row, start, values):
    count, width = values.shape
    high, low = split(values)
    half = parts_ref.shape[0] // 2
    parts_ref[row : row + count, start : start + width] = high
    parts_ref[half + row : half + row + count, start : start + width] = low


def views(fields_ref):
    return fields_ref.at[:16], fields_ref.at[16:32], fields_ref.at[32:33]


def chunks(width):
    return [slice(c, c + STEP) for c in range(0, width, STEP)]


def edges_of(ref, step, low_ref, high_ref):
    @pl.when(step == 0)
    def _():
        high_ref[...] = ref[:, :TILE]

    @pl.when(step == pl.num_programs(0) - 1)
    def _():
        low_ref[...] = ref[:, STEP - TILE :]


def start_kernel(mask_ref, tiles_ref, fields_ref, left_ref, right_ref, *rest):
    ax_ref, other_ref, ax_low, ax_high, parts_ref = rest
    x_ref, p_ref, star_ref = views(fields_ref)
    step, width = pl.program_id(0), fields_ref.shape[1]

    @pl.when(step == 0)
    def _():
        for start, ref in ((0, left_ref), (TILE + width, right_ref)):
            x, p, star = ref[:16], ref[16:32], ref[32:33]
            fill_parts(parts_ref, 0, start, jnp.concatenate([x, x * star, p], axis=0))
        for c in chunks(width):
            x, p = x_ref[:, c], p_ref[:, c]
            fields = jnp.concatenate([x, x * star_ref[:, c], p], axis=0)
            fill_parts(parts_ref, 0, TILE + c.start, fields)

    def store(k, term):
        at = slice(k * TILE, (k + 1) * TILE)
        ax_ref[:, at] = term[:16]
        other_ref[:, at] = term[16:]

    apply_blocks(mask_ref, tiles_ref, parts_ref, store)
    edges_of(ax_ref, step, ax_low, ax_high)


def gram_kernel(mask_ref, tiles_ref, fields_ref, ax_ref, other_ref, *rest):
    left_ref, right_ref, twice_ref, sums_ref, low_ref, high_ref, parts_ref, total_ref, edge_ref = rest
    x_ref, p_ref, star_ref = views(fields_ref)
    step, width = pl.program_id(0), ax_ref.shape[1]

    @pl.when(step == 0)
    def _():
        fill_parts(parts_ref, 0, 0, left_ref[...])
        fill_parts(parts_ref, 0, TILE + width, right_ref[...])
        for c in chunks(width):
            fill_parts(parts_ref, 0, TILE + c.start, ax_ref[:, c])
        total_ref[...] = jnp.zeros_like(total_ref)

    def store(k, term):
        twice_ref[:, k * TILE : (k + 1) * TILE] = term

    apply_blocks(mask_ref, tiles_ref, parts_ref, store)
    here = pl.ds(pl.multiple_of(step * STEP, TILE), STEP)
    x, p, star, ax, other = (r[:, here] for r in (x_ref, p_ref, star_ref, ax_ref, other_ref))
    basis = jnp.concatenate([x, ax, x * star, p], axis=0)
    applied = jnp.concatenate([ax, twice_ref[...], other, basis * star], axis=0)
    total_ref[...] += nt_parts(both_parts(basis), both_parts(applied))
    edge_ref[...] = jnp.concatenate([twice_ref[...], other], axis=0)
    edges_of(edge_ref, step, low_ref, high_ref)

    @pl.when(step == pl.num_programs(0) - 1)
    def _():
        sums = folded(total_ref[...])
        turned = jnp.concatenate([sums, jnp.zeros((64, 128), jnp.float32)], axis=0).T
        turned = jnp.where(lanes(64) < 64, turned[:64], pltpu.roll(turned[64:], 64, 1))
        sums_ref[...] = 0.5 * (sums + turned)


def middle_kernel(mask_ref, tiles_ref, coeffs_ref, ritz_ref, *rest):
    own_refs, left_refs, right_refs = rest[:6], rest[6:9], rest[9:12]
    out_ref, residual_ref, ax_ref, applied_ref, high_ref, parts_ref, all_ref = rest[12:]
    step, width = pl.program_id(0), own_refs[0].shape[1]

    def update(start, x, p, star, ax, twice, other):
        coeffs = coeffs_ref[:, :64]
        pair = nn3(coeffs, jnp.concatenate([x, ax, x * star, p], axis=0))
        applied = nn3(coeffs, jnp.concatenate([ax, twice, other], axis=0))
        x, p = pair[:16], pair[16:]
        mx = x * star
        r = applied[:16] - nn(ritz_ref[...], mx)
        fields = jnp.concatenate([r, applied[16:], mx, r * star, p * star], axis=0)
        fill_parts(parts_ref, 0, start, fields)
        if TILE <= start < TILE + width:
            here = slice(start - TILE, start - TILE + x.shape[1])
            all_ref[:, here] = jnp.concatenate([x, r, p, fields[16:], applied[:16]], axis=0)

    @pl.when(step == 0)
    def _():
        for start, refs in ((0, left_refs), (TILE + width, right_refs)):
            first, ax, last = (r[...] for r in refs)
            update(start, first[:16], first[16:32], first[32:33], ax, last[:16], last[16:])
        for c in chunks(width):
            update(TILE + c.start, *(r[:, c] for r in own_refs))

    def store(k, term):
        at = slice(k * TILE, (k + 1) * TILE)
        residual_ref[:, at] = term[:16]
        applied_ref[:, at] = term[16:]

    apply_blocks(mask_ref, tiles_ref, parts_ref, store)
    here = pl.ds(pl.multiple_of(step * STEP, TILE), STEP)
    out_ref[...] = all_ref[:112, here]
    ax_ref[...] = all_ref[112:, here]

    @pl.when(step == 0)
    def _():
        high_ref[...] = residual_ref[:, :TILE]


def pack_kernel(mask_ref, tiles_ref, star_ref, own_ref, ar_ref, ax_ref, applied_ref, right_ref, *rest):
    sums_ref, parts_ref, stiff_ref, mass_ref = rest
    step, width = pl.program_id(0), star_ref.shape[1]

    @pl.when(step == 0)
    def _():
        fill_parts(parts_ref, 0, width, right_ref[...])
        for c in chunks(width):
            fill_parts(parts_ref, 0, c.start, ar_ref[:, c])
        stiff_ref[...] = jnp.zeros_like(stiff_ref)
        mass_ref[...] = jnp.zeros_like(mass_ref)

    start = pl.multiple_of(step * STEP, TILE)
    window = parts_ref[:, pl.ds(start, STEP + TILE)]
    terms = []
    for k in range(STEP_BLOCKS):
        twofold = 2.0 * weight(mask_ref, step * STEP_BLOCKS + k, 1)
        row = jnp.concatenate([tiles_ref[k, 1], tiles_ref[k, 2] * twofold], axis=1)
        terms.append(folded(nt_parts(window[:, k * TILE : (k + 2) * TILE], both_parts(row))))
    twice = jnp.concatenate(terms, axis=1)
    here = pl.ds(start, STEP)
    own, ar, star = own_ref[:, here], ar_ref[:, here], star_ref[:, here]
    basis = jnp.concatenate([own, ar], axis=0)
    applied = jnp.concatenate(
        [ax_ref[:, here], ar, own[48:64], applied_ref[:, here], twice], axis=0
    )
    left = both_parts(basis)
    stiff_ref[...] += nt_parts(left, both_parts(applied))
    mass_ref[...] += nt_parts(left, both_parts(basis * star))

    @pl.when(step == pl.num_programs(0) - 1)
    def _():
        stiff, mass = folded(stiff_ref[...]), folded(mass_ref[...])
        row, lane = sublanes(128), lanes(128)
        stiff = jnp.where((row >= 112) & (lane >= 112), 0.5 * (stiff + stiff.T), stiff)
        sums_ref[...] = jnp.where(row > lane, stiff, mass)
        along = jnp.sum(jnp.where(row == lane, stiff, 0.0), axis=1, keepdims=True)
        placed = nn(of_groups(8, 128), jnp.where(lane == 64 + row % 16, along, 0.0))
        taken = lanes(8)
        taken = (taken >= 64) & (taken < 80)
        sums_ref[16:24] = jnp.where(taken, placed, sums_ref[16:24])


def of_groups(groups, size):
    row = lax.broadcasted_iota(jnp.int32, (groups, size), 0)
    column = lax.broadcasted_iota(jnp.int32, (groups, size), 1)
    return jnp.where(column // 16 == row, 1.0, 0.0).astype(jnp.float32)


def last_kernel(total_rows, sums_ref, ritz_ref, own_ref, ar_ref, modes_ref, directions_ref, out_ref):
    m = 16
    both = sums_ref[...]
    turned = both.T
    row, lane = sublanes(128), lanes(128)
    group = lax.broadcasted_iota(jnp.int32, (128, 8), 0) // 16
    member = lax.broadcasted_iota(jnp.int32, (128, 8), 1)
    spread = nn(jnp.where(group == member, 1.0, 0.0).astype(jnp.float32), both[16:24])
    along = jnp.sum(jnp.where(lane == 64 + row % 16, spread, 0.0), axis=1, keepdims=True)
    gram_stiff = jnp.where(row > lane, both, jnp.where(row < lane, turned, along))
    gram_mass = jnp.where(row > lane, turned, both)
    of_r = jnp.where((lanes(m) >= 64) & (lanes(m) < 80), pltpu.roll(gram_mass[80:96], 64, 1), gram_mass[16:32])
    of_mx = jnp.where((lanes(m) >= 16) & (lanes(m) < 32), pltpu.roll(gram_mass[:16], 64, 1), gram_mass[64:80])
    gram_mass = jnp.concatenate(
        [gram_mass[:16], of_r, gram_mass[32:64], of_mx, gram_mass[80:]], axis=0
    )
    rotation, ritz_matrix = rayleigh_ritz(
        below(gram_stiff[:48], 48), below(gram_mass[:48], 48), total_rows
    )
    of_x = below(rotation, m)
    of_r = below(rotation, 2 * m) - of_x
    of_p = rotation - of_x - of_r
    wide = nn(rotation[:, :m], jnp.concatenate([ritz_ref[...], jnp.zeros((m, 112), jnp.float32)], axis=1))
    pulled = nn(ritz_matrix, rotation)
    residual = (
        pltpu.roll(of_x, 16, 1)
        + pltpu.roll(of_r, 96, 1)
        + pltpu.roll(of_p, 16, 1)
        + pltpu.roll(wide - pulled, 64, 1)
    )
    basis = jnp.concatenate([rotation, residual, rotation - of_x], axis=0)
    rotation, ritz_matrix = rayleigh_ritz(
        projected(basis, gram_stiff), projected(basis, gram_mass), total_rows
    )
    out_ref[...] = ritz_matrix
    coeffs = pair_coefficients(rotation, basis)
    for c in chunks(own_ref.shape[1]):
        pair = nn3(coeffs, jnp.concatenate([own_ref[:, c], ar_ref[:, c]], axis=0))
        modes_ref[:, c] = pair[:m]
        directions_ref[:, c] = pair[m:]


def shape(*dims):
    return jax.ShapeDtypeStruct(dims, jnp.float32)


def params():
    return pltpu.CompilerParams(vmem_limit_bytes=VMEM)


def on_blocks(kernel, stepped, whole, scratch, mask, tiles, *operands):
    width = tiles.shape[0] * TILE
    return pl.pallas_call(
        kernel,
        grid=(tiles.shape[0] // STEP_BLOCKS,),
        in_specs=[
            pl.BlockSpec(memory_space=pltpu.SMEM),
            pl.BlockSpec((STEP_BLOCKS, 3, TILE, TILE), lambda i: (i, 0, 0, 0)),
        ]
        + [pl.BlockSpec(o.shape, lambda i: (0, 0)) for o in operands],
        out_specs=[pl.BlockSpec((r, STEP), lambda i: (0, i)) for r in stepped]
        + [pl.BlockSpec(w, lambda i: (0, 0)) for w in whole],
        out_shape=[shape(r, width) for r in stepped] + [shape(*w) for w in whole],
        scratch_shapes=scratch,
        compiler_params=params(),
        name=kernel.__name__,
    )(mask, tiles, *operands)


def on_device(stiff_tiles, tile_mask, edge_star, start_modes, start_directions):
    m, width = start_modes.shape
    total_rows = width * lax.axis_size(SLAB)
    star = edge_star[None, :]

    def edge(at):
        tail = jnp.broadcast_to(star[:, at], (8, TILE))
        return jnp.concatenate([start_modes[:, at], start_directions[:, at], tail])

    def parts(rows, halos):
        return pltpu.VMEM((2 * rows, width + halos * TILE), jnp.bfloat16)

    left = [from_left(edge(slice(width - TILE, width)))]
    right = [from_right(edge(slice(0, TILE)))]
    vectors = (start_modes, start_directions, star)
    fields = jnp.concatenate([start_modes, start_directions, jnp.broadcast_to(star, (8, width))])
    applied, other, low, high = on_blocks(
        start_kernel, (m, 2 * m), ((m, TILE),) * 2, [parts(3 * m, 2)],
        tile_mask, stiff_tiles, fields, left[0], right[0],
    )
    left.append(from_left(low))
    right.append(from_right(high))
    twice, sums, low, high = on_blocks(
        gram_kernel, (m,), ((4 * m, 128), (3 * m, TILE), (3 * m, TILE)),
        [parts(m, 2), pltpu.VMEM((8 * m, 256), jnp.float32), pltpu.VMEM((3 * m, STEP), jnp.float32)],
        tile_mask, stiff_tiles, fields, applied, other, left[1], right[1],
    )
    left.append(from_left(low))
    right.append(from_right(high))
    sums = slab_sum(sums)
    coeffs, ritz_matrix = pl.pallas_call(
        functools.partial(first_kernel, total_rows),
        out_shape=(shape(2 * m, 128), shape(m, m)),
        compiler_params=params(),
        name="first_kernel",
    )(sums)
    own, applied_residual, applied, other, high = on_blocks(
        middle_kernel, (7 * m, m, m, 4 * m), ((m, TILE),),
        [parts(5 * m, 2), pltpu.VMEM((8 * m, width), jnp.float32)],
        tile_mask, stiff_tiles, coeffs, ritz_matrix, *vectors, applied, twice, other, *left, *right,
    )
    (sums,) = on_blocks(
        pack_kernel, (), ((8 * m, 128),),
        [parts(m, 1)] + [pltpu.VMEM((16 * m, 256), jnp.float32)] * 2,
        tile_mask, stiff_tiles, star, own, applied_residual, applied, other, from_right(high),
    )
    sums = slab_sum(sums)
    return pl.pallas_call(
        functools.partial(last_kernel, total_rows),
        out_shape=(shape(m, width), shape(m, width), shape(m, m)),
        compiler_params=params(),
        name="last_kernel",
    )(sums, ritz_matrix, own, applied_residual)


def solution(mesh):
    fine = Mesh(mesh.devices.reshape(-1, 4, 2, 4), ("z", "y", "core", "x"))
    in_specs = (
        P(SLAB, None, None, None),
        P(SLAB, None),
        P(SLAB),
        P(None, SLAB),
        P(None, SLAB),
    )
    out_specs = (P(None, SLAB), P(None, SLAB), P())
    return jax.shard_map(
        on_device, mesh=fine, in_specs=in_specs, out_specs=out_specs, check_vma=False
    )
```

```python
import functools

import jax
import jax.numpy as jnp
from jax import lax
from jax.experimental import pallas as pl
from jax.experimental.pallas import tpu as pltpu
from jax.sharding import Mesh
from jax.sharding import PartitionSpec as P

SLAB = ("z", "y", "core")
TILE = 128
STEP_BLOCKS = 16
STEP = STEP_BLOCKS * TILE
VMEM = 20 * 1024 * 1024
WIDTH = 8


def slab_sum(rows):
    parts = lax.axis_size(("y", "core"))
    shared = rows.reshape(parts, -1, 128)
    own = lax.all_to_all(shared, ("y", "core"), 0, 0, tiled=True).sum(0)
    copies = jnp.broadcast_to(own[None], (lax.axis_size("z"),) + own.shape)
    own = lax.all_to_all(copies, "z", 0, 0, tiled=True).sum(0)
    copies = jnp.broadcast_to(own[None], (parts,) + own.shape)
    return lax.all_to_all(copies, ("y", "core"), 0, 0, tiled=True).reshape(rows.shape)


def from_left(edge):
    count = lax.axis_size(SLAB)
    return lax.ppermute(edge, SLAB, [(i, i + 1) for i in range(count - 1)])


def from_right(edge):
    count = lax.axis_size(SLAB)
    return lax.ppermute(edge, SLAB, [(i + 1, i) for i in range(count - 1)])


def split(values):
    high = values.astype(jnp.bfloat16)
    low = (values - high.astype(jnp.float32)).astype(jnp.bfloat16)
    return high, low


def gram(left, right):
    return lax.dot_general(
        left,
        right,
        (((1,), (1,)), ((), ())),
        precision=lax.Precision.HIGHEST,
        preferred_element_type=jnp.float32,
    )


def nn(left, right):
    return jnp.dot(left, right, precision=lax.Precision.HIGHEST, preferred_element_type=jnp.float32)


def nt(left, right):
    return gram(left, right)


def lanes(rows):
    return lax.broadcasted_iota(jnp.int32, (rows, 128), 1)


def sublanes(rows):
    return lax.broadcasted_iota(jnp.int32, (rows, 128), 0)


def diagonal(rows, shift):
    return jnp.where(lanes(rows) == sublanes(rows) + shift, 1.0, 0.0).astype(jnp.float32)


def below(matrix, limit):
    return jnp.where(lanes(matrix.shape[0]) < limit, matrix, 0.0)


def pivots(groups, first, lane, width):
    columns = [
        [jnp.broadcast_to(g[:, lane + j : lane + j + 1], (8, 128)) for g in groups]
        for j in range(width)
    ]

    def spread(values, row):
        return jnp.broadcast_to(values[row // 8][row % 8 : row % 8 + 1], (8, 128))

    block = [[spread(columns[j], first + i) for j in range(width)] for i in range(width)]
    rows = [spread(groups, first + i) for i in range(width)]
    return columns, block, rows


def solved(block, rows):
    width = len(rows)
    block, rows = [list(r) for r in block], list(rows)
    for i in range(width):
        scale = 1.0 / block[i][i]
        block[i] = [v * scale for v in block[i]]
        rows[i] = rows[i] * scale
        for k in range(width):
            if k != i:
                factor = block[k][i]
                for j in range(i + 1, width):
                    block[k][j] = block[k][j] - factor * block[i][j]
                rows[k] = rows[k] - factor * rows[i]
    return rows


def inverse(matrix, size):
    matrix = matrix + diagonal(size, 64)
    groups = [matrix[8 * t : 8 * t + 8] for t in range(size // 8)]
    row = sublanes(8)
    for first in range(0, size, WIDTH):
        columns, block, rows = pivots(groups, first, first, WIDTH)
        rows = solved(block, rows)
        for t in range(size // 8):
            for j in range(WIDTH):
                groups[t] = groups[t] - columns[j][t] * rows[j]
            for j in range(WIDTH):
                if t == (first + j) // 8:
                    groups[t] = jnp.where(row == (first + j) % 8, rows[j], groups[t])
    return jnp.concatenate(groups, axis=0)


def lower_solved(matrix, size, scale):
    groups = [matrix[8 * t : 8 * t + 8] for t in range(size // 8)]
    row = sublanes(8)
    result = [jnp.zeros((8, 128), jnp.float32) for _ in groups]
    for first in range(0, size, WIDTH):
        columns, block, rows = pivots(groups, first, 64 + first, WIDTH)
        whole = solved(block, rows)
        for i in range(WIDTH):
            inverse_root = lax.rsqrt(block[i][i]) * scale
            t, at = (first + i) // 8, (first + i) % 8
            result[t] = jnp.where(row == at, rows[i] * inverse_root, result[t])
            if i + 1 < WIDTH:
                turn = 1.0 / block[i][i]
                for k in range(i + 1, WIDTH):
                    factor = block[k][i] * turn
                    block[k] = [a - factor * b for a, b in zip(block[k], block[i])]
                    rows[k] = rows[k] - factor * rows[i]
        for t in range(size // 8):
            if 8 * t + 7 >= first + WIDTH:
                for j in range(WIDTH):
                    groups[t] = groups[t] - columns[j][t] * whole[j]
    return jnp.concatenate(result, axis=0)


def projected(basis, matrix):
    tall = jnp.concatenate([basis, jnp.zeros((80, 128), jnp.float32)], axis=0)
    return nt(nn(basis[:, : matrix.shape[0]], matrix), tall)


def rayleigh_ritz(gram_stiff, gram_mass, total_rows):
    m, n = 16, 48
    inverted = inverse(gram_stiff + 1.0 * gram_mass, n)
    coeffs = below(pltpu.roll(nn(gram_mass[:m, :n], inverted), 64, 1), n)
    padded = jnp.concatenate(
        [jnp.zeros((64, 128), jnp.float32), coeffs, jnp.zeros((48, 128), jnp.float32)], axis=0
    )
    normalizer = nt(nn(coeffs[:, :n], gram_mass), padded)
    rotation = lower_solved(normalizer + coeffs, m, total_rows**0.5)
    rotation = below(rotation, n)
    ritz_matrix = nt(nn(rotation[:, :n], gram_stiff), rotation) * (1.0 / total_rows)
    return rotation, ritz_matrix


def pair_coefficients(rotation, basis):
    inner = jnp.where(lanes(16) >= 16, rotation, 0.0)
    both = jnp.concatenate([rotation, inner], axis=0)
    return nn(both[:, :48], basis)


def first_kernel(total_rows, sums_ref, coeffs_ref, ritz_ref):
    m = 16
    sums = sums_ref[...]
    gram_stiff = below(sums, 64)
    gram_mass = below(pltpu.roll(sums, 64, 1), 64)
    lane = lanes(m)
    start_mass = jnp.where((lane >= 64) & (lane < 80), sums[:m], 0.0)
    start = below(lower_solved(start_mass + diagonal(m, 0), m, total_rows**0.5), m)
    ritz_matrix = nt(nn(start[:, :m], gram_stiff[:m]), start) * (1.0 / total_rows)
    pulled = nn(ritz_matrix, start)
    residual = pltpu.roll(start, 16, 1) - pltpu.roll(pulled, 32, 1)
    basis = jnp.concatenate([start, residual, diagonal(m, 48)], axis=0)
    rotation, ritz_matrix = rayleigh_ritz(
        projected(basis, gram_stiff), projected(basis, gram_mass), total_rows
    )
    coeffs_ref[...] = pair_coefficients(rotation, basis)
    ritz_ref[...] = ritz_matrix


def nn3(left, right):
    count = left.shape[0]
    left_high, left_low = split(left)
    right_high, right_low = split(right)
    by_high = jnp.dot(
        jnp.concatenate([left_high, left_low], axis=0), right_high, preferred_element_type=jnp.float32
    )
    by_low = jnp.dot(left_high, right_low, preferred_element_type=jnp.float32)
    return by_high[:count] + by_high[count:] + by_low


def both_parts(values):
    return jnp.concatenate(split(values), axis=0)


def nt_parts(left, right):
    return lax.dot_general(left, right, (((1,), (1,)), ((), ())), preferred_element_type=jnp.float32)


def folded(term):
    rows, columns = term.shape[0] // 2, term.shape[1] // 2
    term = term[:, :columns] + term[:, columns:]
    return term[:rows] + term[rows:]


def weight(mask_ref, block, side):
    return mask_ref[block, side].astype(jnp.float32)


def full_rows(mask_ref, tiles_ref, k):
    block = pl.program_id(0) * STEP_BLOCKS + k
    return jnp.concatenate(
        [
            tiles_ref[k, 0] * weight(mask_ref, block, 0),
            tiles_ref[k, 1],
            tiles_ref[k, 2] * weight(mask_ref, block, 1),
        ],
        axis=1,
    )


def apply_blocks(mask_ref, tiles_ref, parts_ref, store):
    start = pl.multiple_of(pl.program_id(0) * STEP, TILE)
    window = parts_ref[:, pl.ds(start, STEP + 2 * TILE)]
    for k in range(STEP_BLOCKS):
        right = both_parts(full_rows(mask_ref, tiles_ref, k))
        store(k, folded(nt_parts(window[:, k * TILE : (k + 3) * TILE], right)))


def fill_parts(parts_ref, row, start, values):
    count, width = values.shape
    high, low = split(values)
    half = parts_ref.shape[0] // 2
    parts_ref[row : row + count, start : start + width] = high
    parts_ref[half + row : half + row + count, start : start + width] = low


def views(fields_ref):
    return fields_ref.at[:16], fields_ref.at[16:32], fields_ref.at[32:33]


def chunks(width):
    return [slice(c, c + STEP) for c in range(0, width, STEP)]


def edges_of(ref, step, low_ref, high_ref):
    @pl.when(step == 0)
    def _():
        high_ref[...] = ref[:, :TILE]

    @pl.when(step == pl.num_programs(0) - 1)
    def _():
        low_ref[...] = ref[:, STEP - TILE :]


def start_kernel(mask_ref, tiles_ref, fields_ref, left_ref, right_ref, *rest):
    ax_ref, other_ref, ax_low, ax_high, parts_ref = rest
    x_ref, p_ref, star_ref = views(fields_ref)
    step, width = pl.program_id(0), fields_ref.shape[1]

    @pl.when(step == 0)
    def _():
        for start, ref in ((0, left_ref), (TILE + width, right_ref)):
            x, p, star = ref[:16], ref[16:32], ref[32:33]
            fill_parts(parts_ref, 0, start, jnp.concatenate([x, x * star, p], axis=0))
        for c in chunks(width):
            x, p = x_ref[:, c], p_ref[:, c]
            fields = jnp.concatenate([x, x * star_ref[:, c], p], axis=0)
            fill_parts(parts_ref, 0, TILE + c.start, fields)

    def store(k, term):
        at = slice(k * TILE, (k + 1) * TILE)
        ax_ref[:, at] = term[:16]
        other_ref[:, at] = term[16:]

    apply_blocks(mask_ref, tiles_ref, parts_ref, store)
    edges_of(ax_ref, step, ax_low, ax_high)


def gram_kernel(mask_ref, tiles_ref, fields_ref, ax_ref, other_ref, *rest):
    left_ref, right_ref, twice_ref, sums_ref, low_ref, high_ref, parts_ref, total_ref, edge_ref = rest
    x_ref, p_ref, star_ref = views(fields_ref)
    step, width = pl.program_id(0), ax_ref.shape[1]

    @pl.when(step == 0)
    def _():
        fill_parts(parts_ref, 0, 0, left_ref[...])
        fill_parts(parts_ref, 0, TILE + width, right_ref[...])
        for c in chunks(width):
            fill_parts(parts_ref, 0, TILE + c.start, ax_ref[:, c])
        total_ref[...] = jnp.zeros_like(total_ref)

    def store(k, term):
        twice_ref[:, k * TILE : (k + 1) * TILE] = term

    apply_blocks(mask_ref, tiles_ref, parts_ref, store)
    here = pl.ds(pl.multiple_of(step * STEP, TILE), STEP)
    x, p, star, ax, other = (r[:, here] for r in (x_ref, p_ref, star_ref, ax_ref, other_ref))
    basis = jnp.concatenate([x, ax, x * star, p], axis=0)
    applied = jnp.concatenate([ax, twice_ref[...], other, basis * star], axis=0)
    total_ref[...] += nt_parts(both_parts(basis), both_parts(applied))
    edge_ref[...] = jnp.concatenate([twice_ref[...], other], axis=0)
    edges_of(edge_ref, step, low_ref, high_ref)

    @pl.when(step == pl.num_programs(0) - 1)
    def _():
        sums = folded(total_ref[...])
        turned = jnp.concatenate([sums, jnp.zeros((64, 128), jnp.float32)], axis=0).T
        turned = jnp.where(lanes(64) < 64, turned[:64], pltpu.roll(turned[64:], 64, 1))
        sums_ref[...] = 0.5 * (sums + turned)


def middle_kernel(mask_ref, tiles_ref, coeffs_ref, ritz_ref, *rest):
    own_refs, left_refs, right_refs = rest[:6], rest[6:9], rest[9:12]
    out_ref, residual_ref, ax_ref, applied_ref, high_ref, parts_ref, all_ref = rest[12:]
    step, width = pl.program_id(0), own_refs[0].shape[1]

    def update(start, x, p, star, ax, twice, other):
        coeffs = coeffs_ref[:, :64]
        pair = nn3(coeffs, jnp.concatenate([x, ax, x * star, p], axis=0))
        applied = nn3(coeffs, jnp.concatenate([ax, twice, other], axis=0))
        x, p = pair[:16], pair[16:]
        mx = x * star
        r = applied[:16] - nn(ritz_ref[...], mx)
        fields = jnp.concatenate([r, applied[16:], mx, r * star, p * star], axis=0)
        fill_parts(parts_ref, 0, start, fields)
        if TILE <= start < TILE + width:
            here = slice(start - TILE, start - TILE + x.shape[1])
            all_ref[:, here] = jnp.concatenate([x, r, p, fields[16:], applied[:16]], axis=0)

    @pl.when(step == 0)
    def _():
        for start, refs in ((0, left_refs), (TILE + width, right_refs)):
            first, ax, last = (r[...] for r in refs)
            update(start, first[:16], first[16:32], first[32:33], ax, last[:16], last[16:])
        for c in chunks(width):
            update(TILE + c.start, *(r[:, c] for r in own_refs))

    def store(k, term):
        at = slice(k * TILE, (k + 1) * TILE)
        residual_ref[:, at] = term[:16]
        applied_ref[:, at] = term[16:]

    apply_blocks(mask_ref, tiles_ref, parts_ref, store)
    here = pl.ds(pl.multiple_of(step * STEP, TILE), STEP)
    out_ref[...] = all_ref[:112, here]
    ax_ref[...] = all_ref[112:, here]

    @pl.when(step == 0)
    def _():
        high_ref[...] = residual_ref[:, :TILE]


def pack_kernel(mask_ref, tiles_ref, star_ref, own_ref, ar_ref, ax_ref, applied_ref, right_ref, *rest):
    sums_ref, parts_ref, stiff_ref, mass_ref = rest
    step, width = pl.program_id(0), star_ref.shape[1]

    @pl.when(step == 0)
    def _():
        fill_parts(parts_ref, 0, width, right_ref[...])
        for c in chunks(width):
            fill_parts(parts_ref, 0, c.start, ar_ref[:, c])
        stiff_ref[...] = jnp.zeros_like(stiff_ref)
        mass_ref[...] = jnp.zeros_like(mass_ref)

    start = pl.multiple_of(step * STEP, TILE)
    window = parts_ref[:, pl.ds(start, STEP + TILE)]
    terms = []
    for k in range(STEP_BLOCKS):
        twofold = 2.0 * weight(mask_ref, step * STEP_BLOCKS + k, 1)
        row = jnp.concatenate([tiles_ref[k, 1], tiles_ref[k, 2] * twofold], axis=1)
        terms.append(folded(nt_parts(window[:, k * TILE : (k + 2) * TILE], both_parts(row))))
    twice = jnp.concatenate(terms, axis=1)
    here = pl.ds(start, STEP)
    own, ar, star = own_ref[:, here], ar_ref[:, here], star_ref[:, here]
    basis = jnp.concatenate([own, ar], axis=0)
    applied = jnp.concatenate(
        [ax_ref[:, here], ar, own[48:64], applied_ref[:, here], twice], axis=0
    )
    left = both_parts(basis)
    stiff_ref[...] += nt_parts(left, both_parts(applied))
    mass_ref[...] += nt_parts(left, both_parts(basis * star))

    @pl.when(step == pl.num_programs(0) - 1)
    def _():
        stiff, mass = folded(stiff_ref[...]), folded(mass_ref[...])
        row, lane = sublanes(128), lanes(128)
        stiff = jnp.where((row >= 112) & (lane >= 112), 0.5 * (stiff + stiff.T), stiff)
        sums_ref[...] = jnp.where(row > lane, stiff, mass)
        along = jnp.sum(jnp.where(row == lane, stiff, 0.0), axis=1, keepdims=True)
        placed = nn(of_groups(8, 128), jnp.where(lane == 64 + row % 16, along, 0.0))
        taken = lanes(8)
        taken = (taken >= 64) & (taken < 80)
        sums_ref[16:24] = jnp.where(taken, placed, sums_ref[16:24])


def of_groups(groups, size):
    row = lax.broadcasted_iota(jnp.int32, (groups, size), 0)
    column = lax.broadcasted_iota(jnp.int32, (groups, size), 1)
    return jnp.where(column // 16 == row, 1.0, 0.0).astype(jnp.float32)


def last_kernel(total_rows, sums_ref, ritz_ref, own_ref, ar_ref, modes_ref, directions_ref, out_ref):
    m = 16
    both = sums_ref[...]
    turned = both.T
    row, lane = sublanes(128), lanes(128)
    group = lax.broadcasted_iota(jnp.int32, (128, 8), 0) // 16
    member = lax.broadcasted_iota(jnp.int32, (128, 8), 1)
    spread = nn(jnp.where(group == member, 1.0, 0.0).astype(jnp.float32), both[16:24])
    along = jnp.sum(jnp.where(lane == 64 + row % 16, spread, 0.0), axis=1, keepdims=True)
    gram_stiff = jnp.where(row > lane, both, jnp.where(row < lane, turned, along))
    gram_mass = jnp.where(row > lane, turned, both)
    of_r = jnp.where((lanes(m) >= 64) & (lanes(m) < 80), pltpu.roll(gram_mass[80:96], 64, 1), gram_mass[16:32])
    of_mx = jnp.where((lanes(m) >= 16) & (lanes(m) < 32), pltpu.roll(gram_mass[:16], 64, 1), gram_mass[64:80])
    gram_mass = jnp.concatenate(
        [gram_mass[:16], of_r, gram_mass[32:64], of_mx, gram_mass[80:]], axis=0
    )
    rotation, ritz_matrix = rayleigh_ritz(
        below(gram_stiff[:48], 48), below(gram_mass[:48], 48), total_rows
    )
    of_x = below(rotation, m)
    of_r = below(rotation, 2 * m) - of_x
    of_p = rotation - of_x - of_r
    wide = nn(rotation[:, :m], jnp.concatenate([ritz_ref[...], jnp.zeros((m, 112), jnp.float32)], axis=1))
    pulled = nn(ritz_matrix, rotation)
    residual = (
        pltpu.roll(of_x, 16, 1)
        + pltpu.roll(of_r, 96, 1)
        + pltpu.roll(of_p, 16, 1)
        + pltpu.roll(wide - pulled, 64, 1)
    )
    basis = jnp.concatenate([rotation, residual, rotation - of_x], axis=0)
    rotation, ritz_matrix = rayleigh_ritz(
        projected(basis, gram_stiff), projected(basis, gram_mass), total_rows
    )
    out_ref[...] = ritz_matrix
    coeffs = pair_coefficients(rotation, basis)
    for c in chunks(own_ref.shape[1]):
        pair = nn3(coeffs, jnp.concatenate([own_ref[:, c], ar_ref[:, c]], axis=0))
        modes_ref[:, c] = pair[:m]
        directions_ref[:, c] = pair[m:]


def shape(*dims):
    return jax.ShapeDtypeStruct(dims, jnp.float32)


def params():
    return pltpu.CompilerParams(vmem_limit_bytes=VMEM)


def on_blocks(kernel, stepped, whole, scratch, mask, tiles, *operands):
    width = tiles.shape[0] * TILE
    return pl.pallas_call(
        kernel,
        grid=(tiles.shape[0] // STEP_BLOCKS,),
        in_specs=[
            pl.BlockSpec(memory_space=pltpu.SMEM),
            pl.BlockSpec((STEP_BLOCKS, 3, TILE, TILE), lambda i: (i, 0, 0, 0)),
        ]
        + [pl.BlockSpec(o.shape, lambda i: (0, 0)) for o in operands],
        out_specs=[pl.BlockSpec((r, STEP), lambda i: (0, i)) for r in stepped]
        + [pl.BlockSpec(w, lambda i: (0, 0)) for w in whole],
        out_shape=[shape(r, width) for r in stepped] + [shape(*w) for w in whole],
        scratch_shapes=scratch,
        compiler_params=params(),
        name=kernel.__name__,
    )(mask, tiles, *operands)


def on_device(stiff_tiles, tile_mask, edge_star, start_modes, start_directions):
    m, width = start_modes.shape
    total_rows = width * lax.axis_size(SLAB)
    star = edge_star[None, :]

    def edge(at):
        tail = jnp.broadcast_to(star[:, at], (8, TILE))
        return jnp.concatenate([start_modes[:, at], start_directions[:, at], tail])

    def parts(rows, halos):
        return pltpu.VMEM((2 * rows, width + halos * TILE), jnp.bfloat16)

    left = [from_left(edge(slice(width - TILE, width)))]
    right = [from_right(edge(slice(0, TILE)))]
    vectors = (start_modes, start_directions, star)
    fields = jnp.concatenate([start_modes, start_directions, jnp.broadcast_to(star, (8, width))])
    applied, other, low, high = on_blocks(
        start_kernel, (m, 2 * m), ((m, TILE),) * 2, [parts(3 * m, 2)],
        tile_mask, stiff_tiles, fields, left[0], right[0],
    )
    left.append(from_left(low))
    right.append(from_right(high))
    twice, sums, low, high = on_blocks(
        gram_kernel, (m,), ((4 * m, 128), (3 * m, TILE), (3 * m, TILE)),
        [parts(m, 2), pltpu.VMEM((8 * m, 256), jnp.float32), pltpu.VMEM((3 * m, STEP), jnp.float32)],
        tile_mask, stiff_tiles, fields, applied, other, left[1], right[1],
    )
    left.append(from_left(low))
    right.append(from_right(high))
    sums = slab_sum(sums)
    coeffs, ritz_matrix = pl.pallas_call(
        functools.partial(first_kernel, total_rows),
        out_shape=(shape(2 * m, 128), shape(m, m)),
        compiler_params=params(),
        name="first_kernel",
    )(sums)
    own, applied_residual, applied, other, high = on_blocks(
        middle_kernel, (7 * m, m, m, 4 * m), ((m, TILE),),
        [parts(5 * m, 2), pltpu.VMEM((8 * m, width), jnp.float32)],
        tile_mask, stiff_tiles, coeffs, ritz_matrix, *vectors, applied, twice, other, *left, *right,
    )
    (sums,) = on_blocks(
        pack_kernel, (), ((8 * m, 128),),
        [parts(m, 1)] + [pltpu.VMEM((16 * m, 256), jnp.float32)] * 2,
        tile_mask, stiff_tiles, star, own, applied_residual, applied, other, from_right(high),
    )
    sums = slab_sum(sums)
    return pl.pallas_call(
        functools.partial(last_kernel, total_rows),
        out_shape=(shape(m, width), shape(m, width), shape(m, m)),
        compiler_params=params(),
        name="last_kernel",
    )(sums, ritz_matrix, own, applied_residual)


def solution(mesh):
    fine = Mesh(mesh.devices.reshape(-1, 4, 2, 4), ("z", "y", "core", "x"))
    in_specs = (
        P(SLAB, None, None, None),
        P(SLAB, None),
        P(SLAB),
        P(None, SLAB),
        P(None, SLAB),
    )
    out_specs = (P(None, SLAB), P(None, SLAB), P())
    return jax.shard_map(
        on_device, mesh=fine, in_specs=in_specs, out_specs=out_specs, check_vma=False
    )
```

```python
import functools

import jax
import jax.numpy as jnp
from jax import lax
from jax.experimental import pallas as pl
from jax.experimental.pallas import tpu as pltpu
from jax.sharding import Mesh
from jax.sharding import PartitionSpec as P

SLAB = ("z", "y", "core")
TILE = 128
STEP_BLOCKS = 32
STEP = STEP_BLOCKS * TILE
VMEM = 20 * 1024 * 1024
WIDTH = 8


def slab_sum(rows):
    parts = lax.axis_size(("y", "core"))
    shared = rows.reshape(parts, -1, 128)
    own = lax.all_to_all(shared, ("y", "core"), 0, 0, tiled=True).sum(0)
    copies = jnp.broadcast_to(own[None], (lax.axis_size("z"),) + own.shape)
    own = lax.all_to_all(copies, "z", 0, 0, tiled=True).sum(0)
    copies = jnp.broadcast_to(own[None], (parts,) + own.shape)
    return lax.all_to_all(copies, ("y", "core"), 0, 0, tiled=True).reshape(rows.shape)


def from_left(edge):
    count = lax.axis_size(SLAB)
    return lax.ppermute(edge, SLAB, [(i, i + 1) for i in range(count - 1)])


def from_right(edge):
    count = lax.axis_size(SLAB)
    return lax.ppermute(edge, SLAB, [(i + 1, i) for i in range(count - 1)])


def split(values):
    high = values.astype(jnp.bfloat16)
    low = (values - high.astype(jnp.float32)).astype(jnp.bfloat16)
    return high, low


def gram(left, right):
    return lax.dot_general(
        left,
        right,
        (((1,), (1,)), ((), ())),
        precision=lax.Precision.HIGHEST,
        preferred_element_type=jnp.float32,
    )


def nn(left, right):
    return jnp.dot(left, right, precision=lax.Precision.HIGHEST, preferred_element_type=jnp.float32)


def nt(left, right):
    return gram(left, right)


def lanes(rows):
    return lax.broadcasted_iota(jnp.int32, (rows, 128), 1)


def sublanes(rows):
    return lax.broadcasted_iota(jnp.int32, (rows, 128), 0)


def diagonal(rows, shift):
    return jnp.where(lanes(rows) == sublanes(rows) + shift, 1.0, 0.0).astype(jnp.float32)


def below(matrix, limit):
    return jnp.where(lanes(matrix.shape[0]) < limit, matrix, 0.0)


def pivots(groups, first, lane, width):
    columns = [
        [jnp.broadcast_to(g[:, lane + j : lane + j + 1], (8, 128)) for g in groups]
        for j in range(width)
    ]

    def spread(values, row):
        return jnp.broadcast_to(values[row // 8][row % 8 : row % 8 + 1], (8, 128))

    block = [[spread(columns[j], first + i) for j in range(width)] for i in range(width)]
    rows = [spread(groups, first + i) for i in range(width)]
    return columns, block, rows


def solved(block, rows):
    width = len(rows)
    block, rows = [list(r) for r in block], list(rows)
    for i in range(width):
        scale = 1.0 / block[i][i]
        block[i] = [v * scale for v in block[i]]
        rows[i] = rows[i] * scale
        for k in range(width):
            if k != i:
                factor = block[k][i]
                for j in range(i + 1, width):
                    block[k][j] = block[k][j] - factor * block[i][j]
                rows[k] = rows[k] - factor * rows[i]
    return rows


def inverse(matrix, size):
    matrix = matrix + diagonal(size, 64)
    groups = [matrix[8 * t : 8 * t + 8] for t in range(size // 8)]
    row = sublanes(8)
    for first in range(0, size, WIDTH):
        columns, block, rows = pivots(groups, first, first, WIDTH)
        rows = solved(block, rows)
        for t in range(size // 8):
            for j in range(WIDTH):
                groups[t] = groups[t] - columns[j][t] * rows[j]
            for j in range(WIDTH):
                if t == (first + j) // 8:
                    groups[t] = jnp.where(row == (first + j) % 8, rows[j], groups[t])
    return jnp.concatenate(groups, axis=0)


def lower_solved(matrix, size, scale):
    groups = [matrix[8 * t : 8 * t + 8] for t in range(size // 8)]
    row = sublanes(8)
    result = [jnp.zeros((8, 128), jnp.float32) for _ in groups]
    for first in range(0, size, WIDTH):
        columns, block, rows = pivots(groups, first, 64 + first, WIDTH)
        whole = solved(block, rows)
        for i in range(WIDTH):
            inverse_root = lax.rsqrt(block[i][i]) * scale
            t, at = (first + i) // 8, (first + i) % 8
            result[t] = jnp.where(row == at, rows[i] * inverse_root, result[t])
            if i + 1 < WIDTH:
                turn = 1.0 / block[i][i]
                for k in range(i + 1, WIDTH):
                    factor = block[k][i] * turn
                    block[k] = [a - factor * b for a, b in zip(block[k], block[i])]
                    rows[k] = rows[k] - factor * rows[i]
        for t in range(size // 8):
            if 8 * t + 7 >= first + WIDTH:
                for j in range(WIDTH):
                    groups[t] = groups[t] - columns[j][t] * whole[j]
    return jnp.concatenate(result, axis=0)


def projected(basis, matrix):
    tall = jnp.concatenate([basis, jnp.zeros((80, 128), jnp.float32)], axis=0)
    return nt(nn(basis[:, : matrix.shape[0]], matrix), tall)


def rayleigh_ritz(gram_stiff, gram_mass, total_rows):
    m, n = 16, 48
    inverted = inverse(gram_stiff + 1.0 * gram_mass, n)
    coeffs = below(pltpu.roll(nn(gram_mass[:m, :n], inverted), 64, 1), n)
    padded = jnp.concatenate(
        [jnp.zeros((64, 128), jnp.float32), coeffs, jnp.zeros((48, 128), jnp.float32)], axis=0
    )
    normalizer = nt(nn(coeffs[:, :n], gram_mass), padded)
    rotation = lower_solved(normalizer + coeffs, m, total_rows**0.5)
    rotation = below(rotation, n)
    ritz_matrix = nt(nn(rotation[:, :n], gram_stiff), rotation) * (1.0 / total_rows)
    return rotation, ritz_matrix


def pair_coefficients(rotation, basis):
    inner = jnp.where(lanes(16) >= 16, rotation, 0.0)
    both = jnp.concatenate([rotation, inner], axis=0)
    return nn(both[:, :48], basis)


def first_kernel(total_rows, sums_ref, coeffs_ref, ritz_ref):
    m = 16
    sums = sums_ref[...]
    gram_stiff = below(sums, 64)
    gram_mass = below(pltpu.roll(sums, 64, 1), 64)
    lane = lanes(m)
    start_mass = jnp.where((lane >= 64) & (lane < 80), sums[:m], 0.0)
    start = below(lower_solved(start_mass + diagonal(m, 0), m, total_rows**0.5), m)
    ritz_matrix = nt(nn(start[:, :m], gram_stiff[:m]), start) * (1.0 / total_rows)
    pulled = nn(ritz_matrix, start)
    residual = pltpu.roll(start, 16, 1) - pltpu.roll(pulled, 32, 1)
    basis = jnp.concatenate([start, residual, diagonal(m, 48)], axis=0)
    rotation, ritz_matrix = rayleigh_ritz(
        projected(basis, gram_stiff), projected(basis, gram_mass), total_rows
    )
    coeffs_ref[...] = pair_coefficients(rotation, basis)
    ritz_ref[...] = ritz_matrix


def nn3(left, right):
    count = left.shape[0]
    left_high, left_low = split(left)
    right_high, right_low = split(right)
    by_high = jnp.dot(
        jnp.concatenate([left_high, left_low], axis=0), right_high, preferred_element_type=jnp.float32
    )
    by_low = jnp.dot(left_high, right_low, preferred_element_type=jnp.float32)
    return by_high[:count] + by_high[count:] + by_low


def both_parts(values):
    return jnp.concatenate(split(values), axis=0)


def nt_parts(left, right):
    return lax.dot_general(left, right, (((1,), (1,)), ((), ())), preferred_element_type=jnp.float32)


def folded(term):
    rows, columns = term.shape[0] // 2, term.shape[1] // 2
    term = term[:, :columns] + term[:, columns:]
    return term[:rows] + term[rows:]


def weight(mask_ref, block, side):
    return mask_ref[block, side].astype(jnp.float32)


def full_rows(mask_ref, tiles_ref, k):
    block = pl.program_id(0) * STEP_BLOCKS + k
    return jnp.concatenate(
        [
            tiles_ref[k, 0] * weight(mask_ref, block, 0),
            tiles_ref[k, 1],
            tiles_ref[k, 2] * weight(mask_ref, block, 1),
        ],
        axis=1,
    )


def apply_blocks(mask_ref, tiles_ref, parts_ref, store):
    start = pl.multiple_of(pl.program_id(0) * STEP, TILE)
    window = parts_ref[:, pl.ds(start, STEP + 2 * TILE)]
    for k in range(STEP_BLOCKS):
        right = both_parts(full_rows(mask_ref, tiles_ref, k))
        store(k, folded(nt_parts(window[:, k * TILE : (k + 3) * TILE], right)))


def fill_parts(parts_ref, row, start, values):
    count, width = values.shape
    high, low = split(values)
    half = parts_ref.shape[0] // 2
    parts_ref[row : row + count, start : start + width] = high
    parts_ref[half + row : half + row + count, start : start + width] = low


def views(fields_ref):
    return fields_ref.at[:16], fields_ref.at[16:32], fields_ref.at[32:33]


def chunks(width):
    return [slice(c, c + STEP) for c in range(0, width, STEP)]


def edges_of(ref, step, low_ref, high_ref):
    @pl.when(step == 0)
    def _():
        high_ref[...] = ref[:, :TILE]

    @pl.when(step == pl.num_programs(0) - 1)
    def _():
        low_ref[...] = ref[:, STEP - TILE :]


def start_kernel(mask_ref, tiles_ref, fields_ref, left_ref, right_ref, *rest):
    ax_ref, other_ref, ax_low, ax_high, parts_ref = rest
    x_ref, p_ref, star_ref = views(fields_ref)
    step, width = pl.program_id(0), fields_ref.shape[1]

    @pl.when(step == 0)
    def _():
        for start, ref in ((0, left_ref), (TILE + width, right_ref)):
            x, p, star = ref[:16], ref[16:32], ref[32:33]
            fill_parts(parts_ref, 0, start, jnp.concatenate([x, x * star, p], axis=0))
        for c in chunks(width):
            x, p = x_ref[:, c], p_ref[:, c]
            fields = jnp.concatenate([x, x * star_ref[:, c], p], axis=0)
            fill_parts(parts_ref, 0, TILE + c.start, fields)

    def store(k, term):
        at = slice(k * TILE, (k + 1) * TILE)
        ax_ref[:, at] = term[:16]
        other_ref[:, at] = term[16:]

    apply_blocks(mask_ref, tiles_ref, parts_ref, store)
    edges_of(ax_ref, step, ax_low, ax_high)


def gram_kernel(mask_ref, tiles_ref, fields_ref, ax_ref, other_ref, *rest):
    left_ref, right_ref, twice_ref, sums_ref, low_ref, high_ref, parts_ref, total_ref, edge_ref = rest
    x_ref, p_ref, star_ref = views(fields_ref)
    step, width = pl.program_id(0), ax_ref.shape[1]

    @pl.when(step == 0)
    def _():
        fill_parts(parts_ref, 0, 0, left_ref[...])
        fill_parts(parts_ref, 0, TILE + width, right_ref[...])
        for c in chunks(width):
            fill_parts(parts_ref, 0, TILE + c.start, ax_ref[:, c])
        total_ref[...] = jnp.zeros_like(total_ref)

    def store(k, term):
        twice_ref[:, k * TILE : (k + 1) * TILE] = term

    apply_blocks(mask_ref, tiles_ref, parts_ref, store)
    here = pl.ds(pl.multiple_of(step * STEP, TILE), STEP)
    x, p, star, ax, other = (r[:, here] for r in (x_ref, p_ref, star_ref, ax_ref, other_ref))
    basis = jnp.concatenate([x, ax, x * star, p], axis=0)
    applied = jnp.concatenate([ax, twice_ref[...], other, basis * star], axis=0)
    total_ref[...] += nt_parts(both_parts(basis), both_parts(applied))
    edge_ref[...] = jnp.concatenate([twice_ref[...], other], axis=0)
    edges_of(edge_ref, step, low_ref, high_ref)

    @pl.when(step == pl.num_programs(0) - 1)
    def _():
        sums = folded(total_ref[...])
        turned = jnp.concatenate([sums, jnp.zeros((64, 128), jnp.float32)], axis=0).T
        turned = jnp.where(lanes(64) < 64, turned[:64], pltpu.roll(turned[64:], 64, 1))
        sums_ref[...] = 0.5 * (sums + turned)


def middle_kernel(mask_ref, tiles_ref, coeffs_ref, ritz_ref, *rest):
    own_refs, left_refs, right_refs = rest[:6], rest[6:9], rest[9:12]
    out_ref, residual_ref, ax_ref, applied_ref, high_ref, parts_ref, all_ref = rest[12:]
    step, width = pl.program_id(0), own_refs[0].shape[1]

    def update(start, x, p, star, ax, twice, other):
        coeffs = coeffs_ref[:, :64]
        pair = nn3(coeffs, jnp.concatenate([x, ax, x * star, p], axis=0))
        applied = nn3(coeffs, jnp.concatenate([ax, twice, other], axis=0))
        x, p = pair[:16], pair[16:]
        mx = x * star
        r = applied[:16] - nn(ritz_ref[...], mx)
        fields = jnp.concatenate([r, applied[16:], mx, r * star, p * star], axis=0)
        fill_parts(parts_ref, 0, start, fields)
        if TILE <= start < TILE + width:
            here = slice(start - TILE, start - TILE + x.shape[1])
            all_ref[:, here] = jnp.concatenate([x, r, p, fields[16:], applied[:16]], axis=0)

    @pl.when(step == 0)
    def _():
        for start, refs in ((0, left_refs), (TILE + width, right_refs)):
            first, ax, last = (r[...] for r in refs)
            update(start, first[:16], first[16:32], first[32:33], ax, last[:16], last[16:])
        for c in chunks(width):
            update(TILE + c.start, *(r[:, c] for r in own_refs))

    def store(k, term):
        at = slice(k * TILE, (k + 1) * TILE)
        residual_ref[:, at] = term[:16]
        applied_ref[:, at] = term[16:]

    apply_blocks(mask_ref, tiles_ref, parts_ref, store)
    here = pl.ds(pl.multiple_of(step * STEP, TILE), STEP)
    out_ref[...] = all_ref[:112, here]
    ax_ref[...] = all_ref[112:, here]

    @pl.when(step == 0)
    def _():
        high_ref[...] = residual_ref[:, :TILE]


def pack_kernel(mask_ref, tiles_ref, star_ref, own_ref, ar_ref, ax_ref, applied_ref, right_ref, *rest):
    sums_ref, parts_ref, stiff_ref, mass_ref = rest
    step, width = pl.program_id(0), star_ref.shape[1]

    @pl.when(step == 0)
    def _():
        fill_parts(parts_ref, 0, width, right_ref[...])
        for c in chunks(width):
            fill_parts(parts_ref, 0, c.start, ar_ref[:, c])
        stiff_ref[...] = jnp.zeros_like(stiff_ref)
        mass_ref[...] = jnp.zeros_like(mass_ref)

    start = pl.multiple_of(step * STEP, TILE)
    window = parts_ref[:, pl.ds(start, STEP + TILE)]
    terms = []
    for k in range(STEP_BLOCKS):
        twofold = 2.0 * weight(mask_ref, step * STEP_BLOCKS + k, 1)
        row = jnp.concatenate([tiles_ref[k, 1], tiles_ref[k, 2] * twofold], axis=1)
        terms.append(folded(nt_parts(window[:, k * TILE : (k + 2) * TILE], both_parts(row))))
    twice = jnp.concatenate(terms, axis=1)
    here = pl.ds(start, STEP)
    own, ar, star = own_ref[:, here], ar_ref[:, here], star_ref[:, here]
    basis = jnp.concatenate([own, ar], axis=0)
    applied = jnp.concatenate(
        [ax_ref[:, here], ar, own[48:64], applied_ref[:, here], twice], axis=0
    )
    left = both_parts(basis)
    stiff_ref[...] += nt_parts(left, both_parts(applied))
    mass_ref[...] += nt_parts(left, both_parts(basis * star))

    @pl.when(step == pl.num_programs(0) - 1)
    def _():
        stiff, mass = folded(stiff_ref[...]), folded(mass_ref[...])
        row, lane = sublanes(128), lanes(128)
        stiff = jnp.where((row >= 112) & (lane >= 112), 0.5 * (stiff + stiff.T), stiff)
        sums_ref[...] = jnp.where(row > lane, stiff, mass)
        along = jnp.sum(jnp.where(row == lane, stiff, 0.0), axis=1, keepdims=True)
        placed = nn(of_groups(8, 128), jnp.where(lane == 64 + row % 16, along, 0.0))
        taken = lanes(8)
        taken = (taken >= 64) & (taken < 80)
        sums_ref[16:24] = jnp.where(taken, placed, sums_ref[16:24])


def of_groups(groups, size):
    row = lax.broadcasted_iota(jnp.int32, (groups, size), 0)
    column = lax.broadcasted_iota(jnp.int32, (groups, size), 1)
    return jnp.where(column // 16 == row, 1.0, 0.0).astype(jnp.float32)


def last_kernel(total_rows, sums_ref, ritz_ref, own_ref, ar_ref, modes_ref, directions_ref, out_ref):
    m = 16
    both = sums_ref[...]
    turned = both.T
    row, lane = sublanes(128), lanes(128)
    group = lax.broadcasted_iota(jnp.int32, (128, 8), 0) // 16
    member = lax.broadcasted_iota(jnp.int32, (128, 8), 1)
    spread = nn(jnp.where(group == member, 1.0, 0.0).astype(jnp.float32), both[16:24])
    along = jnp.sum(jnp.where(lane == 64 + row % 16, spread, 0.0), axis=1, keepdims=True)
    gram_stiff = jnp.where(row > lane, both, jnp.where(row < lane, turned, along))
    gram_mass = jnp.where(row > lane, turned, both)
    of_r = jnp.where((lanes(m) >= 64) & (lanes(m) < 80), pltpu.roll(gram_mass[80:96], 64, 1), gram_mass[16:32])
    of_mx = jnp.where((lanes(m) >= 16) & (lanes(m) < 32), pltpu.roll(gram_mass[:16], 64, 1), gram_mass[64:80])
    gram_mass = jnp.concatenate(
        [gram_mass[:16], of_r, gram_mass[32:64], of_mx, gram_mass[80:]], axis=0
    )
    rotation, ritz_matrix = rayleigh_ritz(
        below(gram_stiff[:48], 48), below(gram_mass[:48], 48), total_rows
    )
    of_x = below(rotation, m)
    of_r = below(rotation, 2 * m) - of_x
    of_p = rotation - of_x - of_r
    wide = nn(rotation[:, :m], jnp.concatenate([ritz_ref[...], jnp.zeros((m, 112), jnp.float32)], axis=1))
    pulled = nn(ritz_matrix, rotation)
    residual = (
        pltpu.roll(of_x, 16, 1)
        + pltpu.roll(of_r, 96, 1)
        + pltpu.roll(of_p, 16, 1)
        + pltpu.roll(wide - pulled, 64, 1)
    )
    basis = jnp.concatenate([rotation, residual, rotation - of_x], axis=0)
    rotation, ritz_matrix = rayleigh_ritz(
        projected(basis, gram_stiff), projected(basis, gram_mass), total_rows
    )
    out_ref[...] = ritz_matrix
    coeffs = pair_coefficients(rotation, basis)
    for c in chunks(own_ref.shape[1]):
        pair = nn3(coeffs, jnp.concatenate([own_ref[:, c], ar_ref[:, c]], axis=0))
        modes_ref[:, c] = pair[:m]
        directions_ref[:, c] = pair[m:]


def shape(*dims):
    return jax.ShapeDtypeStruct(dims, jnp.float32)


def params():
    return pltpu.CompilerParams(vmem_limit_bytes=VMEM)


def on_blocks(kernel, stepped, whole, scratch, mask, tiles, *operands):
    width = tiles.shape[0] * TILE
    return pl.pallas_call(
        kernel,
        grid=(tiles.shape[0] // STEP_BLOCKS,),
        in_specs=[
            pl.BlockSpec(memory_space=pltpu.SMEM),
            pl.BlockSpec((STEP_BLOCKS, 3, TILE, TILE), lambda i: (i, 0, 0, 0)),
        ]
        + [pl.BlockSpec(o.shape, lambda i: (0, 0)) for o in operands],
        out_specs=[pl.BlockSpec((r, STEP), lambda i: (0, i)) for r in stepped]
        + [pl.BlockSpec(w, lambda i: (0, 0)) for w in whole],
        out_shape=[shape(r, width) for r in stepped] + [shape(*w) for w in whole],
        scratch_shapes=scratch,
        compiler_params=params(),
        name=kernel.__name__,
    )(mask, tiles, *operands)


def on_device(stiff_tiles, tile_mask, edge_star, start_modes, start_directions):
    m, width = start_modes.shape
    total_rows = width * lax.axis_size(SLAB)
    star = edge_star[None, :]

    def edge(at):
        tail = jnp.broadcast_to(star[:, at], (8, TILE))
        return jnp.concatenate([start_modes[:, at], start_directions[:, at], tail])

    def parts(rows, halos):
        return pltpu.VMEM((2 * rows, width + halos * TILE), jnp.bfloat16)

    left = [from_left(edge(slice(width - TILE, width)))]
    right = [from_right(edge(slice(0, TILE)))]
    vectors = (start_modes, start_directions, star)
    fields = jnp.concatenate([start_modes, start_directions, jnp.broadcast_to(star, (8, width))])
    applied, other, low, high = on_blocks(
        start_kernel, (m, 2 * m), ((m, TILE),) * 2, [parts(3 * m, 2)],
        tile_mask, stiff_tiles, fields, left[0], right[0],
    )
    left.append(from_left(low))
    right.append(from_right(high))
    twice, sums, low, high = on_blocks(
        gram_kernel, (m,), ((4 * m, 128), (3 * m, TILE), (3 * m, TILE)),
        [parts(m, 2), pltpu.VMEM((8 * m, 256), jnp.float32), pltpu.VMEM((3 * m, STEP), jnp.float32)],
        tile_mask, stiff_tiles, fields, applied, other, left[1], right[1],
    )
    left.append(from_left(low))
    right.append(from_right(high))
    sums = slab_sum(sums)
    coeffs, ritz_matrix = pl.pallas_call(
        functools.partial(first_kernel, total_rows),
        out_shape=(shape(2 * m, 128), shape(m, m)),
        compiler_params=params(),
        name="first_kernel",
    )(sums)
    own, applied_residual, applied, other, high = on_blocks(
        middle_kernel, (7 * m, m, m, 4 * m), ((m, TILE),),
        [parts(5 * m, 2), pltpu.VMEM((8 * m, width), jnp.float32)],
        tile_mask, stiff_tiles, coeffs, ritz_matrix, *vectors, applied, twice, other, *left, *right,
    )
    (sums,) = on_blocks(
        pack_kernel, (), ((8 * m, 128),),
        [parts(m, 1)] + [pltpu.VMEM((16 * m, 256), jnp.float32)] * 2,
        tile_mask, stiff_tiles, star, own, applied_residual, applied, other, from_right(high),
    )
    sums = slab_sum(sums)
    return pl.pallas_call(
        functools.partial(last_kernel, total_rows),
        out_shape=(shape(m, width), shape(m, width), shape(m, m)),
        compiler_params=params(),
        name="last_kernel",
    )(sums, ritz_matrix, own, applied_residual)


def solution(mesh):
    fine = Mesh(mesh.devices.reshape(-1, 4, 2, 4), ("z", "y", "core", "x"))
    in_specs = (
        P(SLAB, None, None, None),
        P(SLAB, None),
        P(SLAB),
        P(None, SLAB),
        P(None, SLAB),
    )
    out_specs = (P(None, SLAB), P(None, SLAB), P())
    return jax.shard_map(
        on_device, mesh=fine, in_specs=in_specs, out_specs=out_specs, check_vma=False
    )
```
